512 devices in a mesh: wide: 64 (over z, x), col: 8 (over y, core).
Axes of the slice: x: 4, y: 4, z: 16, core: 2. Of those that a mesh axis runs over, the one named last changes fastest.
Arguments:
- phi_values: bfloat16 [64, 8, 8, 384, 512], P('wide', 'col'), may hold values from -1.5 to 1.5
- density: bfloat16 [128, 16, 128, 128], P('wide', 'col'), may hold values from -3.5 to 3.5
- lnv_matrix: bfloat16 [128, 16, 128, 128], P('wide', 'col'), may hold values from -0.1875 to 0.1875
- core_density: float32 [128, 128, 128], P('wide', 'col'), may hold values from 0.5 to 2
- pair_owner: int32 [64, 8, 72, 1], P('wide', 'col'), may hold values from 0 to 63; in each aligned block of 72 rows (0 to 71, 72 to 143, ..., all dimensions but the last counted through in order) at most 2 rows name the same one
- pair_source: int32 [64, 8, 72], P('wide', 'col'), may hold values from 0 to 3
- term_left: int32 [128, 16, 8], P('wide', 'col'), may hold values from 0 to 15
- term_right: int32 [128, 16, 8], P('wide', 'col'), may hold values from 0 to 11
Outputs:
- potential: float32 [128, 128, 128], P('wide', 'col')
- hamiltonian: float32 [128, 16, 128, 128], P('wide', 'col')
- gradient: float32 [128, 16, 128, 128], P('wide', 'col')
The draws below stay inside these ranges and needn't reach their ends.
Inputs may be any that keep to these rules, and one draw needn't show every extreme that they name: `pair_owner`: within the 72 pairs of one device no owner is named more than 2 times, and some device names some owner exactly 2 times.
All inputs are finite; a program needn't handle non-finite values.
Results may differ from the reference program's by a relative error of at most 0.0051.
Values may be sent and summed in bfloat16 or wider, within the bound.
A program may use at most 64 MiB of HBM per device.

```python
import math
import jax
import jax.numpy as jnp
import numpy as np
from jax import lax

OB = 128
TILES_DEV = 8
TX = 2
TY = 16
TZT = 16
BR_DEV = 2
NZ_DEV = 2
NTERM = 8
NLOC = 4
NBLK = 128
NNZ = 16
SLABS = 64
STRIPS = 8
NPAIR = 72
CAP = 2
TZ = 128
PT = 512
NX = 128
NY = 128
N_WIDE = 64


def plant(values, stream_key, low, high):
    extent = values.shape
    place = [jax.random.randint(jax.random.fold_in(stream_key, axis), (), 0, extent[axis]) for axis in range(len(extent))]
    values = values.at[tuple(place)].set(low)
    longest = extent.index(max(extent))
    place[longest] = (place[longest] + 1) % extent[longest]
    return values.at[tuple(place)].set(high)


def block_levels(key, extent, cuts, low, largest):
    gain = 1.0
    for position, shards_of in cuts:
        steps = jax.random.uniform(jax.random.fold_in(jax.random.fold_in(key, 6), position), (shards_of,), jnp.float32, low / len(cuts), largest / len(cuts))
        gain = gain * jnp.repeat(jnp.exp(steps), extent[position] // shards_of).reshape((-1,) + (1,) * (len(extent) - 1 - position))
    return gain


def deal_out(key, own, number, rows, count, top, most, skew):
    sequence = jax.random.permutation(key, count)
    heavy_load, common = load_shares(count, rows * top, most, skew, True), load_shares(count, rows * top, most, skew, False)
    places = jnp.arange(count)

    def named(sizes, turn):
        used = int((sizes > 0).sum())
        fixed = max(1, used // 4)
        shifted = fixed + (places - fixed + turn * (used - fixed)) % max(1, count - fixed)
        return jnp.zeros((count,), jnp.int32).at[sequence[jnp.where(places < fixed, places, shifted)]].set(jnp.asarray(sizes, jnp.int32))

    sizes = jnp.where(number % 4 == 0, named(heavy_load, number // 4), named(common, number - number // 4 - 1))
    mixed = jax.random.permutation(jax.random.fold_in(own, 3), count)
    source_of, receiver = mixed[0:count // 2 * 2:2], mixed[1:count // 2 * 2:2]
    slack = jnp.minimum(sizes[source_of] - 1, most - sizes[receiver]) // 2
    slack = jnp.where((source_of == sequence[0]) | (receiver == sequence[0]) | (sizes[receiver] == 0), 0, jnp.maximum(slack, 0))
    shifted = jax.random.randint(jax.random.fold_in(own, 4), (count // 2,), 0, 1 << 20) % (slack + 1)
    sizes = sizes.at[source_of].add(-shifted).at[receiver].add(shifted)
    items = jnp.searchsorted(jnp.cumsum(sizes), jnp.arange(rows * top), side="right").astype(jnp.int32)
    listing = items.reshape(top, rows).T
    listing = listing[jax.random.permutation(jax.random.fold_in(own, 1), rows)]
    turn = jax.random.randint(jax.random.fold_in(own, 2), (rows, 1), 0, top)
    return jnp.take_along_axis(listing, (jnp.arange(top)[None, :] + turn) % top, axis=1)


def load_shares(amount, total, limit, lean, full):
    portions = [(1 << 20) // math.isqrt(standing ** lean) + 1 for standing in range(1, amount + 1)]
    largest = limit if full else min(limit, max(-(-total // amount), total * portions[0] // sum(portions)))
    least = 1 if total - largest >= amount - 1 else 0
    counts, rest = [largest] + [least] * (amount - 1), total - largest - least * (amount - 1)
    while rest > 0:
        candidates = [i for i in range(1, amount) if counts[i] < largest] or [i for i in range(1, amount) if counts[i] < limit]
        pool, remaining = sum([portions[i] for i in candidates]), rest
        for i in candidates:
            more = min(limit - counts[i], max(1, remaining * portions[i] // pool), rest)
            counts[i] = counts[i] + more
            rest = rest - more
    return np.array(counts)


def centred(key, shape, spread, most, cuts=(), kind=jnp.bfloat16):
    array = spread * jax.random.normal(key, shape, jnp.float32)
    if cuts:
        array = array * block_levels(key, shape, cuts, -0.22, 0.18)
    return jnp.clip(array, -most, most).astype(kind)


def setup_inputs(seed: int = 0) -> dict:
    splits = jax.random.split(jax.random.key(seed), 9)
    phi_values = centred(splits[0], (SLABS, STRIPS, TILES_DEV, 3 * OB, PT), (0.5 / (TX * TY * TZT) ** 0.25), 1.5, ((0, 64), (1, 8)))
    density = centred(splits[1], (NBLK, NNZ, OB, OB), (4.0 * (TX * TY * TZT) ** 0.5 / (3 * OB)), 3.5, ((0, 64), (1, 8)))
    lnv_matrix = centred(splits[2], (NBLK, NNZ, OB, OB), (NTERM * OB) ** -0.5, 0.1875, ((0, 64), (1, 8)))
    core_density = jnp.clip(jnp.exp(math.log(2.0) - 1.3862944 * jax.random.uniform(splits[3], (NX, NY, TZ), jnp.float32) ** block_levels(splits[3], (NX, NY, TZ), ((0, 64), (1, 8)), -0.2, 0.2)), 0.5, 2.0)
    pair_owner_keys = jax.random.split(jax.random.fold_in(splits[4], 1), SLABS * STRIPS * NPAIR // NPAIR)
    pair_owner_turns = jax.random.permutation(jax.random.fold_in(splits[4], 3), SLABS * STRIPS * NPAIR // NPAIR)
    pair_owner = jax.vmap(lambda own, number: deal_out(jax.random.fold_in(splits[4], 2), own, number, NPAIR, N_WIDE, 1, CAP, 2))(pair_owner_keys, pair_owner_turns).reshape((SLABS, STRIPS, NPAIR, 1))
    pair_source = plant(jax.random.randint(splits[5], (SLABS, STRIPS, NPAIR), 0, NLOC), jax.random.fold_in(splits[5], 1), 0, NLOC - 1).astype(jnp.int32)
    term_left = plant(jax.random.randint(splits[6], (NBLK, NNZ, NTERM), 0, NNZ), jax.random.fold_in(splits[6], 1), 0, NNZ - 1).astype(jnp.int32)
    term_right = plant(jax.random.randint(splits[7], (NBLK, NNZ, NTERM), 0, 3 * NLOC), jax.random.fold_in(splits[7], 1), 0, (3 * NLOC) - 1).astype(jnp.int32)
    return {"phi_values": phi_values, "density": density, "lnv_matrix": lnv_matrix, "core_density": core_density, "pair_owner": pair_owner, "pair_source": pair_source, "term_left": term_left, "term_right": term_right}


SPACING = 0.1
ENHANCE_LIMIT = 0.804
GRADIENT_COEFF = 0.2195

def exchange_energy(smooth, grad_sq):
    fermi_sq = (3.0 * jnp.pi ** 2) ** (2.0 / 3.0)
    reduced = grad_sq / (4.0 * fermi_sq * smooth ** (8.0 / 3.0))
    enhance = 1.0 + ENHANCE_LIMIT - ENHANCE_LIMIT / (1.0 + GRADIENT_COEFF * reduced / ENHANCE_LIMIT)
    return -0.75 * (3.0 / jnp.pi) ** (1.0 / 3.0) * smooth ** (4.0 / 3.0) * enhance

def total_energy(charge, core_density):
    smooth = jnp.sqrt(charge * charge + core_density * core_density)
    grad_sq = jnp.zeros_like(charge)
    for axis_id in range(3):
        slope = (jnp.roll(charge, -1, axis_id) - jnp.roll(charge, 1, axis_id)) / (2.0 * SPACING)
        grad_sq = grad_sq + slope * slope
    return jnp.sum(exchange_energy(smooth, grad_sq))

def block_place(owners, sources, strip):
    row_index = owners * BR_DEV + sources // NZ_DEV
    slot_index = strip * NZ_DEV + sources % NZ_DEV
    return (row_index, slot_index)

def tiles_to_field(values):
    return values.reshape(TILES_DEV, TX, TY, TZT).transpose(1, 2, 0, 3).reshape(TX, TY, TZ)

def field_to_tiles(field):
    return field.reshape(TX, TY, TILES_DEV, TZT).transpose(2, 0, 1, 3).reshape(TILES_DEV, PT)

def sparse_product(left_blocks, right_blocks, term_left, term_right):
    slot_strip = jnp.arange(NNZ, dtype=jnp.int32) // NZ_DEV

    def one_row(inputs):
        row_id, left_row, lefts, rights = inputs
        window_row = (row_id // BR_DEV * BR_DEV - BR_DEV + rights // NZ_DEV) % NBLK
        window_slot = slot_strip[:, None] * NZ_DEV + rights % NZ_DEV
        chosen_right = right_blocks[window_row, window_slot].astype(jnp.float32)
        chosen_left = left_row[lefts].astype(jnp.float32)
        return jnp.einsum('jtab,jtbc->jac', chosen_left, chosen_right, precision=lax.Precision.HIGHEST)
    return lax.map(one_row, (jnp.arange(NBLK, dtype=jnp.int32), left_blocks, term_left, term_right))

def reference(phi_values, density, lnv_matrix, core_density, pair_owner, pair_source, term_left, term_right):
    devices = SLABS * STRIPS
    phi_all = phi_values.reshape(devices, TILES_DEV, 3 * OB, PT)
    owners = pair_owner.reshape(devices, NPAIR)
    sources = pair_source.reshape(devices, NPAIR)
    strips = jnp.arange(devices, dtype=jnp.int32) % STRIPS

    def grid_density(inputs):
        orbital_values, owner_row, source_row, strip = inputs
        row_index, slot_index = block_place(owner_row, source_row, strip)
        blocks = density[row_index, slot_index]
        tile_matrix = blocks.reshape(TILES_DEV, 3, 3, OB, OB).transpose(0, 1, 3, 2, 4).reshape(TILES_DEV, 3 * OB, 3 * OB)
        values = orbital_values.astype(jnp.float32)
        applied = jnp.einsum('tij,tjp->tip', tile_matrix.astype(jnp.float32), values, precision=lax.Precision.HIGHEST)
        return tiles_to_field(lax.optimization_barrier(jnp.sum(values * applied, axis=1)))
    fields = lax.map(grid_density, (phi_all, owners, sources, strips))
    charge = fields.reshape(SLABS, STRIPS, TX, TY, TZ).transpose(0, 2, 1, 3, 4).reshape(NX, NY, TZ)
    potential = jax.grad(total_energy)(charge, core_density)
    local_pot = potential.reshape(SLABS, TX, STRIPS, TY, TZ).transpose(0, 2, 1, 3, 4).reshape(devices, TX, TY, TZ)

    def add_parts(hamiltonian, inputs):
        orbital_values, owner_row, source_row, strip, field = inputs
        voltage = field_to_tiles(field)
        values = orbital_values.astype(jnp.float32)
        weighted = (values * voltage[:, None, :]).astype(jnp.bfloat16)
        tile_ham = jnp.einsum('tip,tjp->tij', weighted.astype(jnp.float32), values, precision=lax.Precision.HIGHEST)
        pieces = tile_ham.reshape(TILES_DEV, 3, OB, 3, OB).transpose(0, 1, 3, 2, 4).reshape(NPAIR, OB, OB)
        pieces = lax.optimization_barrier(pieces.astype(jnp.bfloat16)).astype(jnp.float32)
        row_index, slot_index = block_place(owner_row, source_row, strip)
        return (hamiltonian.at[row_index, slot_index].add(pieces), None)
    hamiltonian, _ = lax.scan(add_parts, jnp.zeros((NBLK, NNZ, OB, OB), jnp.float32), (phi_all, owners, sources, strips, local_pot))
    first_term = sparse_product(lnv_matrix, hamiltonian.astype(jnp.bfloat16), term_left, term_right)
    second = sparse_product(lnv_matrix, first_term.astype(jnp.bfloat16), term_left, term_right)
    gradient = 3.0 * first_term - 2.0 * second
    return (potential, hamiltonian, gradient)
```

```python
import functools
import math

import jax
import jax.numpy as jnp
from jax import lax
from jax.experimental import pallas as pl
from jax.experimental.pallas import tpu as pltpu
from jax.sharding import PartitionSpec as P

MESH = pl.DeviceIdType.MESH
NX = 4
SPACING = 0.1
KAPPA = 0.804
MU = 0.2195
FERMI_SQ = (3.0 * math.pi**2) ** (2.0 / 3.0)
AMPLITUDE = 0.75 * (3.0 / math.pi) ** (1.0 / 3.0)
ROWS = 32


def place_arrays(owners, sources, depth):
    me = lax.axis_index("wide")
    pairs = owners.shape[0]
    order = jnp.arange(pairs, dtype=jnp.int32)
    dz = jnp.mod(owners // NX - me // NX, depth)
    dx = jnp.mod(owners % NX - me % NX, NX)
    same = (owners[:, None] == owners[None, :]) & (order[None, :] < order[:, None])
    seat = jnp.sum(same.astype(jnp.int32), axis=1)
    slot = dx * (2 * depth) + dz * 2 + seat
    slots = jnp.arange(2 * NX * depth, dtype=jnp.int32)
    hit = slot[:, None] == slots[None, :]
    slot_pair = jnp.sum(jnp.where(hit, order[:, None] - pairs, 0), axis=0) + pairs
    slot_source = jnp.sum(jnp.where(hit, sources[:, None] + 1, 0), axis=0) - 1
    entry = jnp.where(
        dx == 0,
        dz * 4 + sources,
        jnp.where(
            dx == 3,
            4 * depth + dz * 3 + seat,
            jnp.where(dx == 1, 7 * depth + dz * 3 + seat, 10 * depth + seat * depth + dz),
        ),
    )
    return slot_pair, slot_source, entry


def step_kernel(
    depth,
    slot_pair,
    entry,
    left_at,
    right_at,
    req,
    dens,
    lnv,
    core,
    phi_hbm,
    pot_out,
    ham_out,
    grad_out,
    phi,
    want,
    buf,
    xsend,
    parts,
    rsend,
    rleft,
    rright,
    rfleft,
    rfright,
    zin,
    zout,
    lnv_all,
    lnv_cat,
    tile_matrix,
    charge,
    halo,
    flux,
    halo2,
    window,
    window2,
    ham_half,
    first_half,
    phi_sem,
    want_sem,
    lnv_sem,
    z_sem,
    x_sem,
    f_sem,
    rx_sem,
    rf_sem,
    rz_sem,
    halo_sem,
    win_sem,
):
    w = lax.axis_index("wide")
    c = lax.axis_index("col")
    wides = depth * NX
    cols = lax.axis_size("col")
    tiles = charge.shape[0]
    half = depth // 2
    ob = dens.shape[1]
    z, x = lax.div(w, NX), lax.rem(w, NX)

    def chip(dz, dx):
        return (lax.rem(z + depth + dz, depth) * NX + lax.rem(x + NX + dx, NX), c)

    zup, zdn, xr, xl, x2 = chip(1, 0), chip(-1, 0), chip(0, 1), chip(0, -1), chip(0, 2)
    wp = (lax.rem(w + 1, wides), c)
    wm = (lax.rem(w + wides - 1, wides), c)
    strip = [(w, lax.rem(c + d, cols)) for d in range(1, cols)]
    cp, cm = strip[0], strip[-1]

    def remote(src, dst, sems, index, device):
        return pltpu.make_async_remote_copy(
            src_ref=src,
            dst_ref=dst,
            send_sem=sems.at[(0, *index)],
            recv_sem=sems.at[(1, *index)],
            device_id=device,
            device_id_type=MESH,
        )

    phi_copy = pltpu.make_async_copy(phi_hbm, phi, phi_sem)
    phi_copy.start()

    barrier = pltpu.get_barrier_semaphore()
    greeted = [zup, zdn, xr, xl, x2, wp, wm, *strip]
    for device in greeted:
        pl.semaphore_signal(barrier, inc=1, device_id=device, device_id_type=MESH)
    pl.semaphore_wait(barrier, len(greeted))

    left0, right0, fleft0, fright0 = 4 * depth, 7 * depth, 10 * depth, 11 * depth
    span = 2 * depth

    def z_copy(k, way, lo=0, hi=4):
        if way == 0:
            j = lax.rem(depth - k, depth)
            return remote(
                buf.at[pl.ds(4 * j + lo, hi - lo)],
                buf.at[pl.ds(4 * (depth - k - 1) + lo, hi - lo)],
                z_sem, (0, k), zup,
            )
        return remote(
            buf.at[pl.ds(4 * k + lo, hi - lo)], buf.at[pl.ds(4 * k + 4 + lo, hi - lo)], z_sem, (1, k), zdn
        )

    def x_copy(j, way):
        if way == 0:
            return remote(xsend.at[0, j], buf.at[pl.ds(left0 + 3 * j, 3)], x_sem, (0, j), xr)
        return remote(xsend.at[1, j], buf.at[pl.ds(right0 + 3 * j, 3)], x_sem, (1, j), xl)

    def f_copy(j, way):
        if way == 0:
            return remote(buf.at[left0 + 3 * j + 2], buf.at[fleft0 + j], f_sem, (0, j), xr)
        return remote(buf.at[right0 + 3 * j + 2], buf.at[fright0 + j], f_sem, (1, j), xl)

    def pack(j):
        wanted = (((3, 0), (3, 1), (2, 0)), ((1, 0), (1, 1), (2, 1)))
        for lo in range(0, ob, ROWS):
            rows = pl.ds(lo, ROWS)
            b = [buf[4 * j + s, rows, :].astype(jnp.float32) for s in range(4)]
            for way in range(2):
                for n, (dx, seat) in enumerate(wanted[way]):
                    src = want[pl.ds(dx * span + 2 * j + seat, 1), :]
                    got = jnp.where(
                        src == 0, b[0], jnp.where(src == 1, b[1], jnp.where(src == 2, b[2], b[3]))
                    )
                    xsend[way, j, n, rows, :] = got.astype(jnp.bfloat16)
        for way in range(2):
            x_copy(j, way).start()

    def forward(j):
        for way in range(2):
            x_copy(j, way).wait_recv()
            f_copy(j, way).start()

    def want_copy(dx, device):
        rows = pl.ds(dx * span, span)
        return remote(req.at[rows], want.at[rows], want_sem, (dx,), device)

    for s in range(4):
        buf[s] = dens[s]
    want_copies = [want_copy(1, xr), want_copy(3, xl), want_copy(2, x2)]
    for copy in want_copies:
        copy.start()
    for way in range(2):
        z_copy(0, way).start()

    def lnv_copy(d):
        return remote(lnv, lnv_all.at[pl.ds(4 * (cols - d), 4)], lnv_sem, (d,), strip[d - 1])

    for d in range(1, cols):
        lnv_copy(d).start()
    for s in range(4):
        lnv_all[s] = lnv[s]
    want[pl.ds(0, span), :] = req[pl.ds(0, span), :]
    for copy in want_copies:
        copy.wait_recv()
    pack(0)

    def gather_step(k, carry):
        for way in range(2):
            z_copy(k - 1, way).wait_recv()
            z_copy(k, way).start()
        pack(depth - k)
        pack(k)

        @pl.when(k == 2)
        def _():
            forward(0)

        @pl.when(k > 2)
        def _():
            forward(depth - k + 2)
            forward(k - 2)

        return carry

    lax.fori_loop(1, half - 1, gather_step, 0)
    for way in range(2):
        z_copy(half - 2, way).wait_recv()
        z_copy(half - 1, way, 2 * way, 2 * way + 2).start()
    pack(half + 1)
    pack(half - 1)
    for k in range(half - 3, half - 1):
        if k == 0:
            forward(0)
        elif k > 0:
            forward(depth - k)
            forward(k)
    for way in range(2):
        z_copy(half - 1, way, 2 * way, 2 * way + 2).wait_recv()
    pack(half)
    forward(half + 1)
    forward(half - 1)
    forward(half)

    def gather_end(j, carry):
        for way in range(2):
            f_copy(j, way).wait_recv()
        return carry

    lax.fori_loop(0, depth, gather_end, 0)
    phi_copy.wait()

    def charge_step(t, carry):
        for a in range(3):
            for b in range(3):
                tile_matrix[pl.ds(ob * a, ob), pl.ds(ob * b, ob)] = buf[entry[9 * t + 3 * a + b]]
        values = phi[t]
        applied = jnp.dot(tile_matrix[...], values, preferred_element_type=jnp.float32)
        charge[pl.ds(t, 1), :] = jnp.sum(values.astype(jnp.float32) * applied, axis=0, keepdims=True)
        return carry

    lax.fori_loop(0, tiles, charge_step, 0)

    sides = (wp, wm, cp, cm)

    def halo_copy(src, dst, first, n):
        return remote(src, dst.at[n], halo_sem, (first + n,), sides[n])

    for n in range(4):
        halo_copy(charge, halo, 0, n).start()

    points = charge.shape[1]
    xcell, ycell, zcell = points // 2, points // 32, 1
    lane = lax.broadcasted_iota(jnp.int32, (tiles, points), 1)
    at_x = lax.div(lane, xcell)
    at_y = lax.rem(lax.div(lane, ycell), 16)
    at_z = lax.rem(lane, 16)

    def turned(a, shift):
        return pltpu.roll(a, shift % points, 1)

    def x_next(a, beyond):
        return turned(jnp.where(at_x == 1, a, beyond), xcell)

    def x_prev(a, beyond):
        return turned(jnp.where(at_x == 0, a, beyond), xcell)

    def y_next(a, beyond):
        return jnp.where(at_y < 15, turned(a, -ycell), turned(beyond, 15 * ycell))

    def y_prev(a, beyond):
        return jnp.where(at_y > 0, turned(a, ycell), turned(beyond, -15 * ycell))

    def z_next(a):
        return jnp.where(at_z < 15, turned(a, -1), turned(pltpu.roll(a, tiles - 1, 0), 15))

    def z_prev(a):
        return jnp.where(at_z > 0, turned(a, 1), turned(pltpu.roll(a, 1, 0), -15))

    rho = charge[...]
    for n in range(4):
        halo_copy(charge, halo, 0, n).wait_recv()
    grad_x = (x_next(rho, halo[1]) - x_prev(rho, halo[0])) / (2.0 * SPACING)
    grad_y = (y_next(rho, halo[3]) - y_prev(rho, halo[2])) / (2.0 * SPACING)
    grad_z = (z_next(rho) - z_prev(rho)) / (2.0 * SPACING)
    sigma = grad_x * grad_x + grad_y * grad_y + grad_z * grad_z
    n_sq = rho * rho + core[...] * core[...]
    third = jnp.exp(jnp.log(n_sq) * (1.0 / 6.0))
    smooth = jnp.sqrt(n_sq)
    four_thirds = smooth * third
    s2 = sigma / (4.0 * FERMI_SQ * four_thirds * four_thirds)
    denom = 1.0 + MU * s2 / KAPPA
    enhance = 1.0 + KAPPA - KAPPA / denom
    slope = MU / (denom * denom)
    de_dn = -AMPLITUDE * third * ((4.0 / 3.0) * enhance - (8.0 / 3.0) * s2 * slope)
    de_dsigma = -AMPLITUDE * slope / (4.0 * FERMI_SQ * four_thirds)
    flux_x = 2.0 * de_dsigma * grad_x
    flux_y = 2.0 * de_dsigma * grad_y
    flux_z = 2.0 * de_dsigma * grad_z
    flux[0] = flux_x
    flux[1] = flux_y
    for n in range(4):
        halo_copy(flux.at[n // 2], halo2, 4, n).start()
    partial = de_dn * rho / smooth + (z_prev(flux_z) - z_next(flux_z)) / (2.0 * SPACING)
    for n in range(4):
        halo_copy(flux.at[n // 2], halo2, 4, n).wait_recv()
    divergence = (
        x_prev(flux_x, halo2[0])
        - x_next(flux_x, halo2[1])
        + y_prev(flux_y, halo2[2])
        - y_next(flux_y, halo2[3])
    )
    pot_out[...] = partial + divergence / (2.0 * SPACING)

    parts[9 * tiles] = jnp.zeros((ob, ob), jnp.bfloat16)

    def part_step(t, carry):
        values = phi[t]
        weighted = (values.astype(jnp.float32) * pot_out[pl.ds(t, 1), :]).astype(jnp.bfloat16)
        block = lax.dot_general(
            weighted, values, (((1,), (1,)), ((), ())), preferred_element_type=jnp.float32
        ).astype(jnp.bfloat16)
        for a in range(3):
            for b in range(3):
                parts[9 * t + 3 * a + b] = block[ob * a : ob * a + ob, ob * b : ob * b + ob]
        return carry

    lax.fori_loop(0, tiles, part_step, 0)

    def rx_copy(j, way):
        return remote(rsend.at[way, j], (rleft, rright)[way].at[j], rx_sem, (way, j), (xr, xl)[way])

    def rf_copy(j, way):
        return remote(
            (rleft, rright)[way].at[j, 2], (rfleft, rfright)[way].at[j], rf_sem, (way, j), (xr, xl)[way]
        )

    def rz_copy(k, way, lo=0, hi=4):
        rows = pl.ds(lo, hi - lo)
        return remote(zout.at[way, k, rows], zin.at[way, k, rows], rz_sem, (way, k), (zup, zdn)[way])

    def give(j):
        slots = (((1, 0), (1, 1), (2, 0)), ((3, 0), (3, 1), (2, 1)))
        for way in range(2):
            for n, (dx, seat) in enumerate(slots[way]):
                rsend[way, j, n] = parts[slot_pair[dx * span + 2 * j + seat]]
            rx_copy(j, way).start()

    def pass_on(j):
        for way in range(2):
            rx_copy(j, way).wait_recv()
            rf_copy(j, way).start()

    def summed(j, lo):
        rows = pl.ds(lo, ROWS)
        pieces = [
            (0, 0, parts[slot_pair[2 * j], rows, :]),
            (0, 1, parts[slot_pair[2 * j + 1], rows, :]),
            (1, 0, rleft[j, 0, rows, :]),
            (1, 1, rleft[j, 1, rows, :]),
            (3, 0, rright[j, 0, rows, :]),
            (3, 1, rright[j, 1, rows, :]),
            (2, 0, rfleft[j, rows, :]),
            (2, 1, rfright[j, rows, :]),
        ]
        total = [jnp.zeros((ROWS, ob), jnp.float32)] * 4
        for dx, seat, piece in pieces:
            src = want[pl.ds(dx * span + 2 * j + seat, 1), :]
            piece = piece.astype(jnp.float32)
            total = [t + jnp.where(src == s, piece, 0.0) for s, t in enumerate(total)]
        return total

    def arrived(j):
        for way in range(2):
            rf_copy(j, way).wait_recv()

    for s in range(2):
        zin[0, 0, 2 + s] = jnp.zeros((ob, ob), jnp.bfloat16)
        zin[1, 0, s] = jnp.zeros((ob, ob), jnp.bfloat16)
    give(half)
    give(half - 1)
    give(half + 1)
    pass_on(half)
    give(half - 2)
    give(half + 2)
    pass_on(half - 1)
    pass_on(half + 1)
    arrived(half)
    for lo in range(0, ob, ROWS):
        total = summed(half, lo)
        for s in range(4):
            zout[s // 2, 0, s, pl.ds(lo, ROWS), :] = total[s].astype(jnp.bfloat16)
    for way in range(2):
        rz_copy(0, way, 2 * way, 2 * way + 2).start()

    def reduce_step(k, carry):
        @pl.when(k < half - 2)
        def _():
            give(half - k - 2)
            give(half + k + 2)

        @pl.when(k == half - 2)
        def _():
            give(0)

        @pl.when(k < half - 1)
        def _():
            pass_on(half - k - 1)
            pass_on(half + k + 1)

        @pl.when(k == half - 1)
        def _():
            pass_on(0)

        for way in range(2):
            j = half - k if way == 0 else half + k
            arrived(j)

            @pl.when(k == 1)
            def _():
                rz_copy(0, way, 2 * way, 2 * way + 2).wait_recv()

            @pl.when(k > 1)
            def _():
                rz_copy(k - 1, way).wait_recv()

            for lo in range(0, ob, ROWS):
                rows = pl.ds(lo, ROWS)
                total = summed(j, lo)
                for s in range(4):
                    zout[way, k, s, rows, :] = (
                        total[s] + zin[way, k - 1, s, rows, :].astype(jnp.float32)
                    ).astype(jnp.bfloat16)
            rz_copy(k, way).start()
        return carry

    lax.fori_loop(1, half, reduce_step, 0)

    for d in range(1, cols):
        lnv_copy(d).wait_recv()

    def left_step(n, carry):
        for t in range(8):
            lnv_cat[n, :, pl.ds(ob * t, ob)] = lnv_all[left_at[8 * n + t]]
        return carry

    lax.fori_loop(0, 4, left_step, 0)
    arrived(0)
    for way in range(2):
        rz_copy(half - 1, way).wait_recv()
    for lo in range(0, ob, ROWS):
        rows = pl.ds(lo, ROWS)
        total = summed(0, lo)
        for s in range(4):
            value = (
                total[s]
                + zin[0, half - 1, s, rows, :].astype(jnp.float32)
                + zin[1, half - 1, s, rows, :].astype(jnp.float32)
            )
            ham_out[s, rows, :] = value
            ham_half[s, rows, :] = value.astype(jnp.bfloat16)

    def win_copy(src, dst, first, n):
        return remote(src, dst.at[pl.ds(8 * n, 4)], win_sem, (first + n,), (wp, wm)[n])

    def product(n, win):
        chosen = jnp.concatenate([win[right_at[8 * n + t]] for t in range(8)], axis=0)
        return jnp.dot(lnv_cat[n], chosen, preferred_element_type=jnp.float32)

    for n in range(2):
        win_copy(ham_half, window, 0, n).start()
    for s in range(4):
        window[4 + s] = ham_half[s]
    for n in range(2):
        win_copy(ham_half, window, 0, n).wait_recv()
    for n in range(4):
        first = product(n, window)
        grad_out[n] = first
        first_half[n] = first.astype(jnp.bfloat16)
    for n in range(2):
        win_copy(first_half, window2, 2, n).start()
    for s in range(4):
        window2[4 + s] = first_half[s]
    for n in range(2):
        win_copy(first_half, window2, 2, n).wait_recv()
    for n in range(4):
        grad_out[n] = 3.0 * grad_out[n] - 2.0 * product(n, window2)

    for copy in want_copies:
        copy.wait_send()
    for d in range(1, cols):
        lnv_copy(d).wait_send()
    for n in range(4):
        halo_copy(charge, halo, 0, n).wait_send()
        halo_copy(flux.at[n // 2], halo2, 4, n).wait_send()
    for n in range(2):
        win_copy(ham_half, window, 0, n).wait_send()
        win_copy(first_half, window2, 2, n).wait_send()
    for way in range(2):
        z_copy(half - 1, way, 2 * way, 2 * way + 2).wait_send()
        rz_copy(0, way, 2 * way, 2 * way + 2).wait_send()

    def sent_x(j, carry):
        for way in range(2):
            x_copy(j, way).wait_send()
            f_copy(j, way).wait_send()
            rx_copy(j, way).wait_send()
            rf_copy(j, way).wait_send()
        return carry

    def sent_z(k, carry):
        for way in range(2):
            z_copy(k, way).wait_send()
            rz_copy(k + 1, way).wait_send()
        return carry

    lax.fori_loop(0, depth, sent_x, 0)
    lax.fori_loop(0, half - 1, sent_z, 0)


def body(phi_values, density, lnv_matrix, core_density, pair_owner, pair_source, term_left, term_right):
    phi = phi_values[0, 0]
    tiles, _, points = phi.shape
    ob = density.shape[-1]
    depth = lax.axis_size("wide") // NX
    cols = lax.axis_size("col")
    half = depth // 2
    slot_pair, slot_source, entry = place_arrays(pair_owner[0, 0, :, 0], pair_source[0, 0], depth)
    req = jnp.broadcast_to(slot_source[:, None], (2 * NX * depth, ob))
    row = jnp.arange(2, dtype=jnp.int32)[:, None, None]
    left_at = jnp.mod(term_left // 2 - lax.axis_index("col"), cols) * 4 + row * 2 + term_left % 2
    slabs, strips, deep = core_density.shape
    core = (
        core_density.reshape(slabs, strips, tiles, deep // tiles).transpose(2, 0, 1, 3).reshape(tiles, points)
    )
    block = lambda *n: pltpu.VMEM((*n, ob, ob), jnp.bfloat16)
    sems = lambda *n: pltpu.SemaphoreType.DMA((2, *n))
    vmem = pl.BlockSpec(memory_space=pltpu.VMEM)
    smem = pl.BlockSpec(memory_space=pltpu.SMEM)
    pot, ham, grad = pl.pallas_call(
        functools.partial(step_kernel, depth),
        out_shape=(
            jax.ShapeDtypeStruct((tiles, points), jnp.float32),
            jax.ShapeDtypeStruct((4, ob, ob), jnp.float32),
            jax.ShapeDtypeStruct((4, ob, ob), jnp.float32),
        ),
        in_specs=[smem] * 4 + [vmem] * 4 + [pl.BlockSpec(memory_space=pl.ANY)],
        out_specs=(vmem, vmem, vmem),
        scratch_shapes=[
            pltpu.VMEM(phi.shape, jnp.bfloat16),
            pltpu.VMEM(req.shape, jnp.int32),
            block(12 * depth),
            block(2, depth, 3),
            block(9 * tiles + 1),
            block(2, depth, 3),
            block(depth, 3),
            block(depth, 3),
            block(depth),
            block(depth),
            block(2, half, 4),
            block(2, half, 4),
            block(4 * cols),
            pltpu.VMEM((4, ob, 8 * ob), jnp.bfloat16),
            pltpu.VMEM((3 * ob, 3 * ob), jnp.bfloat16),
            pltpu.VMEM((tiles, points), jnp.float32),
            pltpu.VMEM((4, tiles, points), jnp.float32),
            pltpu.VMEM((2, tiles, points), jnp.float32),
            pltpu.VMEM((4, tiles, points), jnp.float32),
            block(12),
            block(12),
            block(4),
            block(4),
            pltpu.SemaphoreType.DMA,
            sems(4),
            sems(cols),
            sems(2, half),
            sems(2, depth),
            sems(2, depth),
            sems(2, depth),
            sems(2, depth),
            sems(2, half),
            sems(8),
            sems(4),
        ],
        compiler_params=pltpu.CompilerParams(
            collective_id=0, has_side_effects=True, vmem_limit_bytes=48 * 1024 * 1024
        ),
    )(
        slot_pair,
        entry,
        left_at.reshape(-1),
        term_right.reshape(-1),
        req,
        density.reshape(4, ob, ob),
        lnv_matrix.reshape(4, ob, ob),
        core,
        phi,
    )
    potential = (
        pot.reshape(tiles, slabs, strips, deep // tiles).transpose(1, 2, 0, 3).reshape(slabs, strips, deep)
    )
    return potential, ham.reshape(density.shape), grad.reshape(density.shape)


def solution(mesh):
    grid = lambda n: P("wide", "col", *([None] * n))
    return jax.shard_map(
        body,
        mesh=mesh,
        in_specs=(grid(3), grid(2), grid(2), grid(1), grid(2), grid(1), grid(1), grid(1)),
        out_specs=(grid(1), grid(2), grid(2)),
        check_vma=False,
    )
```

```python
import functools
import math

import jax
import jax.numpy as jnp
from jax import lax
from jax.experimental import pallas as pl
from jax.experimental.pallas import tpu as pltpu
from jax.sharding import PartitionSpec as P

MESH = pl.DeviceIdType.MESH
NX = 4
SPACING = 0.1
KAPPA = 0.804
MU = 0.2195
FERMI_SQ = (3.0 * math.pi**2) ** (2.0 / 3.0)
AMPLITUDE = 0.75 * (3.0 / math.pi) ** (1.0 / 3.0)
ROWS = 32


def place_arrays(owners, sources, depth):
    me = lax.axis_index("wide")
    pairs = owners.shape[0]
    order = jnp.arange(pairs, dtype=jnp.int32)
    dz = jnp.mod(owners // NX - me // NX, depth)
    dx = jnp.mod(owners % NX - me % NX, NX)
    same = (owners[:, None] == owners[None, :]) & (order[None, :] < order[:, None])
    seat = jnp.sum(same.astype(jnp.int32), axis=1)
    slot = dx * (2 * depth) + dz * 2 + seat
    slots = jnp.arange(2 * NX * depth, dtype=jnp.int32)
    hit = slot[:, None] == slots[None, :]
    slot_pair = jnp.sum(jnp.where(hit, order[:, None] - pairs, 0), axis=0) + pairs
    slot_source = jnp.sum(jnp.where(hit, sources[:, None] + 1, 0), axis=0) - 1
    part = jnp.arange(2, dtype=jnp.int32)[None, :]
    dz, dx, seat, sources = dz[:, None], dx[:, None], seat[:, None], sources[:, None]
    near = dz * 5 + seat * 2 + part
    far = jnp.where(part == 0, 20 * depth + dz * 4 + sources, 18 * depth + seat * depth + dz)
    entry = jnp.where(
        dx == 0,
        dz * 8 + part * 4 + sources,
        jnp.where(dx == 3, 8 * depth + near, jnp.where(dx == 1, 13 * depth + near, far)),
    ).reshape(-1)
    return slot_pair, slot_source, entry


def step_kernel(
    depth,
    slot_pair,
    entry,
    left_at,
    right_at,
    req,
    dens,
    lnv,
    core,
    phi_hbm,
    pot_out,
    ham_out,
    grad_out,
    phi,
    want,
    buf,
    xsend,
    parts,
    rsend,
    rleft,
    rright,
    rfleft,
    rfright,
    zin,
    zout,
    far_in,
    far_out,
    lnv_all,
    lnv_cat,
    tile_matrix,
    charge,
    halo,
    flux,
    halo2,
    window,
    window2,
    ham_half,
    first_half,
    phi_sem,
    want_sem,
    lnv_sem,
    z_sem,
    x_sem,
    f_sem,
    rx_sem,
    rf_sem,
    rz_sem,
    halo_sem,
    win_sem,
):
    w = lax.axis_index("wide")
    c = lax.axis_index("col")
    wides = depth * NX
    cols = lax.axis_size("col")
    tiles = charge.shape[0]
    half = depth // 2
    ob = phi.shape[1] // 3
    hb = ob // 2
    z, x = lax.div(w, NX), lax.rem(w, NX)

    def chip(dz, dx):
        return (lax.rem(z + depth + dz, depth) * NX + lax.rem(x + NX + dx, NX), c)

    zup, zdn, xr, xl, x2 = chip(1, 0), chip(-1, 0), chip(0, 1), chip(0, -1), chip(0, 2)
    wp = (lax.rem(w + 1, wides), c)
    wm = (lax.rem(w + wides - 1, wides), c)
    strip = [(w, lax.rem(c + d, cols)) for d in range(1, cols)]
    cp, cm = strip[0], strip[-1]

    def remote(src, dst, sems, index, device):
        return pltpu.make_async_remote_copy(
            src_ref=src,
            dst_ref=dst,
            send_sem=sems.at[(0, *index)],
            recv_sem=sems.at[(1, *index)],
            device_id=device,
            device_id_type=MESH,
        )

    phi_copy = pltpu.make_async_copy(phi_hbm, phi, phi_sem)
    phi_copy.start()

    barrier = pltpu.get_barrier_semaphore()
    greeted = [zup, zdn, xr, xl, x2, wp, wm, *strip]
    for device in greeted:
        pl.semaphore_signal(barrier, inc=1, device_id=device, device_id_type=MESH)
    pl.semaphore_wait(barrier, len(greeted))

    left0, right0, fleft0, fright0, far0 = 8 * depth, 13 * depth, 18 * depth, 19 * depth, 20 * depth
    span = 2 * depth

    def z_copy(chain, k, way, lo=0, hi=4):
        stride, base = (8, 0) if chain == 0 else (8, 4) if chain == 1 else (4, far0)
        if way == 0:
            src, dst = lax.rem(depth - k, depth), depth - k - 1
        else:
            src, dst = k, k + 1
        return remote(
            buf.at[pl.ds(stride * src + base + lo, hi - lo)],
            buf.at[pl.ds(stride * dst + base + lo, hi - lo)],
            z_sem, (chain, way, k), (zup, zdn)[way],
        )

    def z_first(chain):
        for way in range(2):
            z_copy(chain, 0, way).start()

    def z_step(chain, k):
        for way in range(2):
            z_copy(chain, k - 1, way).wait_recv()
            z_copy(chain, k, way).start()

    def z_half(chain):
        for way in range(2):
            z_copy(chain, half - 2, way).wait_recv()
            z_copy(chain, half - 1, way, 2 * way, 2 * way + 2).start()

    def z_last(chain):
        for way in range(2):
            z_copy(chain, half - 1, way, 2 * way, 2 * way + 2).wait_recv()

    def x_copy(j, way):
        if way == 0:
            return remote(xsend.at[0, j], buf.at[pl.ds(left0 + 5 * j, 5)], x_sem, (0, j), xr)
        return remote(xsend.at[1, j], buf.at[pl.ds(right0 + 5 * j, 5)], x_sem, (1, j), xl)

    def f_copy(j, way):
        if way == 0:
            return remote(buf.at[left0 + 5 * j + 4], buf.at[fleft0 + j], f_sem, (0, j), xr)
        return remote(buf.at[right0 + 5 * j + 4], buf.at[fright0 + j], f_sem, (1, j), xl)

    def pack(j):
        wanted = (((3, 0), (3, 1), (2, 0)), ((1, 0), (1, 1), (2, 1)))
        for h in range(2):
            for lo in range(0, hb, ROWS):
                rows = pl.ds(lo, ROWS)
                b = [buf[8 * j + 4 * h + s, rows, :].astype(jnp.float32) for s in range(4)]
                for way in range(2):
                    for n, (dx, seat) in enumerate(wanted[way]):
                        if n == 2 and h == 0:
                            continue
                        src = want[pl.ds(dx * span + 2 * j + seat, 1), :]
                        got = jnp.where(
                            src == 0, b[0], jnp.where(src == 1, b[1], jnp.where(src == 2, b[2], b[3]))
                        )
                        xsend[way, j, 4 if n == 2 else 2 * n + h, rows, :] = got.astype(jnp.bfloat16)
        for way in range(2):
            x_copy(j, way).start()

    def forward(j):
        for way in range(2):
            x_copy(j, way).wait_recv()
            f_copy(j, way).start()

    def want_copy(dx, device):
        rows = pl.ds(dx * span, span)
        return remote(req.at[rows], want.at[rows], want_sem, (dx,), device)

    for s in range(8):
        buf[s] = dens[s // 4 + 2 * (s % 4)]
    want_copies = [want_copy(1, xr), want_copy(3, xl), want_copy(2, x2)]
    for copy in want_copies:
        copy.start()
    far_copy = remote(buf.at[pl.ds(0, 4)], buf.at[pl.ds(far0, 4)], want_sem, (0,), x2)
    far_copy.start()
    z_first(0)
    z_first(1)

    def lnv_copy(d):
        return remote(lnv, lnv_all.at[pl.ds(4 * (cols - d), 4)], lnv_sem, (d,), strip[d - 1])

    for d in range(1, cols):
        lnv_copy(d).start()
    for s in range(4):
        lnv_all[s] = lnv[s]
    want[pl.ds(0, span), :] = req[pl.ds(0, span), :]
    for copy in want_copies:
        copy.wait_recv()
    pack(0)
    far_copy.wait_recv()
    z_first(2)

    def gather_step(k, carry):
        z_step(0, k)
        z_step(1, k)
        pack(depth - k)
        pack(k)
        z_step(2, k)

        @pl.when(k == 2)
        def _():
            forward(0)

        @pl.when(k > 2)
        def _():
            forward(depth - k + 2)
            forward(k - 2)

        return carry

    lax.fori_loop(1, half - 1, gather_step, 0)
    z_half(0)
    z_half(1)
    pack(half + 1)
    pack(half - 1)
    z_half(2)
    for k in range(half - 3, half - 1):
        if k == 0:
            forward(0)
        elif k > 0:
            forward(depth - k)
            forward(k)
    z_last(0)
    z_last(1)
    pack(half)
    forward(half + 1)
    forward(half - 1)
    forward(half)
    z_last(2)

    def gather_end(j, carry):
        for way in range(2):
            f_copy(j, way).wait_recv()
        return carry

    lax.fori_loop(0, depth, gather_end, 0)
    phi_copy.wait()

    def gather_sent():
        def sent_x(j, carry):
            for way in range(2):
                x_copy(j, way).wait_send()
                f_copy(j, way).wait_send()
            return carry

        def sent_z(k, carry):
            for chain in range(3):
                for way in range(2):
                    z_copy(chain, k, way).wait_send()
            return carry

        for copy in want_copies:
            copy.wait_send()
        far_copy.wait_send()
        for d in range(1, cols):
            lnv_copy(d).wait_send()
        for chain in range(3):
            for way in range(2):
                z_copy(chain, half - 1, way, 2 * way, 2 * way + 2).wait_send()
        lax.fori_loop(0, depth, sent_x, 0)
        lax.fori_loop(0, half - 1, sent_z, 0)


    def charge_step(t, carry):
        for a in range(3):
            for b in range(3):
                for h in range(2):
                    tile_matrix[pl.ds(ob * a + hb * h, hb), pl.ds(ob * b, ob)] = buf[
                        entry[18 * t + 6 * a + 2 * b + h]
                    ]
        values = phi[t]
        applied = jnp.dot(tile_matrix[...], values, preferred_element_type=jnp.float32)
        charge[pl.ds(t, 1), :] = jnp.sum(values.astype(jnp.float32) * applied, axis=0, keepdims=True)
        return carry

    lax.fori_loop(0, tiles, charge_step, 0)

    sides = (wp, wm, cp, cm)

    def halo_copy(src, dst, first, n):
        return remote(src, dst.at[n], halo_sem, (first + n,), sides[n])

    for n in range(4):
        halo_copy(charge, halo, 0, n).start()

    points = charge.shape[1]
    xcell, ycell, zcell = points // 2, points // 32, 1
    lane = lax.broadcasted_iota(jnp.int32, (tiles, points), 1)
    at_x = lax.div(lane, xcell)
    at_y = lax.rem(lax.div(lane, ycell), 16)
    at_z = lax.rem(lane, 16)

    def turned(a, shift):
        return pltpu.roll(a, shift % points, 1)

    def x_next(a, beyond):
        return turned(jnp.where(at_x == 1, a, beyond), xcell)

    def x_prev(a, beyond):
        return turned(jnp.where(at_x == 0, a, beyond), xcell)

    def y_next(a, beyond):
        return jnp.where(at_y < 15, turned(a, -ycell), turned(beyond, 15 * ycell))

    def y_prev(a, beyond):
        return jnp.where(at_y > 0, turned(a, ycell), turned(beyond, -15 * ycell))

    def z_next(a):
        return jnp.where(at_z < 15, turned(a, -1), turned(pltpu.roll(a, tiles - 1, 0), 15))

    def z_prev(a):
        return jnp.where(at_z > 0, turned(a, 1), turned(pltpu.roll(a, 1, 0), -15))

    rho = charge[...]
    for n in range(4):
        halo_copy(charge, halo, 0, n).wait_recv()
    grad_x = (x_next(rho, halo[1]) - x_prev(rho, halo[0])) / (2.0 * SPACING)
    grad_y = (y_next(rho, halo[3]) - y_prev(rho, halo[2])) / (2.0 * SPACING)
    grad_z = (z_next(rho) - z_prev(rho)) / (2.0 * SPACING)
    sigma = grad_x * grad_x + grad_y * grad_y + grad_z * grad_z
    n_sq = rho * rho + core[...] * core[...]
    third = jnp.exp(jnp.log(n_sq) * (1.0 / 6.0))
    smooth = jnp.sqrt(n_sq)
    four_thirds = smooth * third
    s2 = sigma / (4.0 * FERMI_SQ * four_thirds * four_thirds)
    denom = 1.0 + MU * s2 / KAPPA
    enhance = 1.0 + KAPPA - KAPPA / denom
    slope = MU / (denom * denom)
    de_dn = -AMPLITUDE * third * ((4.0 / 3.0) * enhance - (8.0 / 3.0) * s2 * slope)
    de_dsigma = -AMPLITUDE * slope / (4.0 * FERMI_SQ * four_thirds)
    flux_x = 2.0 * de_dsigma * grad_x
    flux_y = 2.0 * de_dsigma * grad_y
    flux_z = 2.0 * de_dsigma * grad_z
    flux[0] = flux_x
    flux[1] = flux_y
    for n in range(4):
        halo_copy(flux.at[n // 2], halo2, 4, n).start()
    partial = de_dn * rho / smooth + (z_prev(flux_z) - z_next(flux_z)) / (2.0 * SPACING)
    for n in range(4):
        halo_copy(flux.at[n // 2], halo2, 4, n).wait_recv()
    divergence = (
        x_prev(flux_x, halo2[0])
        - x_next(flux_x, halo2[1])
        + y_prev(flux_y, halo2[2])
        - y_next(flux_y, halo2[3])
    )
    pot_out[...] = partial + divergence / (2.0 * SPACING)

    def halo_sent():
        for n in range(4):
            halo_copy(charge, halo, 0, n).wait_send()
            halo_copy(flux.at[n // 2], halo2, 4, n).wait_send()

    parts[9 * tiles] = jnp.zeros((ob, ob), jnp.bfloat16)

    def part_step(t, carry):
        values = phi[t]
        weighted = (values.astype(jnp.float32) * pot_out[pl.ds(t, 1), :]).astype(jnp.bfloat16)
        block = lax.dot_general(
            weighted, values, (((1,), (1,)), ((), ())), preferred_element_type=jnp.float32
        ).astype(jnp.bfloat16)
        for a in range(3):
            for b in range(3):
                parts[9 * t + 3 * a + b] = block[ob * a : ob * a + ob, ob * b : ob * b + ob]
        return carry

    lax.fori_loop(0, tiles, part_step, 0)

    def rx_copy(j, way):
        return remote(rsend.at[way, j], (rleft, rright)[way].at[j], rx_sem, (way, j), (xr, xl)[way])

    def rf_copy(j, way):
        return remote(
            (rleft, rright)[way].at[j, 4], (rfleft, rfright)[way].at[j], rf_sem, (way, j), (xr, xl)[way]
        )

    def rz_copy(chain, k, way, lo=0, hi=4):
        rows = pl.ds(lo, hi - lo)
        return remote(
            zout.at[way, k, chain, rows], zin.at[way, k, chain, rows], rz_sem, (chain, way, k), (zup, zdn)[way]
        )

    def give(j):
        slots = (((1, 0), (1, 1), (2, 0)), ((3, 0), (3, 1), (2, 1)))
        for way in range(2):
            for n, (dx, seat) in enumerate(slots[way]):
                pair = slot_pair[dx * span + 2 * j + seat]
                if n < 2:
                    rsend[way, j, 2 * n] = parts[pair, :hb, :]
                    rsend[way, j, 2 * n + 1] = parts[pair, hb:, :]
                else:
                    rsend[way, j, 4] = parts[pair, hb:, :]
            rx_copy(j, way).start()

    def pass_on(j):
        for way in range(2):
            rx_copy(j, way).wait_recv()
            rf_copy(j, way).start()

    def by_source(pieces, j):
        total = [jnp.zeros((ROWS, ob), jnp.float32)] * 4
        for ref, dx, seat, piece in pieces:
            src = ref[pl.ds(dx * span + 2 * j + seat, 1), :]
            piece = piece.astype(jnp.float32)
            total = [t + jnp.where(src == s, piece, 0.0) for s, t in enumerate(total)]
        return total

    def summed(j, chain, lo):
        rows = pl.ds(lo, ROWS)
        if chain == 2:
            return by_source(
                [(req, 2, s, parts[slot_pair[2 * span + 2 * j + s], rows, :]) for s in range(2)], j
            )
        pieces = [
            (req, 0, s, parts[slot_pair[2 * j + s], pl.ds(hb * chain + lo, ROWS), :]) for s in range(2)
        ]
        for s in range(2):
            pieces.append((want, 1, s, rleft[j, 2 * s + chain, rows, :]))
            pieces.append((want, 3, s, rright[j, 2 * s + chain, rows, :]))
        if chain == 1:
            pieces.append((want, 2, 0, rfleft[j, rows, :]))
            pieces.append((want, 2, 1, rfright[j, rows, :]))
        return by_source(pieces, j)

    def arrived(j):
        for way in range(2):
            rf_copy(j, way).wait_recv()

    def rz_first(chain):
        for lo in range(0, hb, ROWS):
            total = summed(half, chain, lo)
            for s in range(4):
                zout[s // 2, 0, chain, s, pl.ds(lo, ROWS), :] = total[s].astype(jnp.bfloat16)
        for way in range(2):
            rz_copy(chain, 0, way, 2 * way, 2 * way + 2).start()

    def rz_arrived(chain, k, way):
        @pl.when(k == 0)
        def _():
            rz_copy(chain, 0, way, 2 * way, 2 * way + 2).wait_recv()

        @pl.when(k > 0)
        def _():
            rz_copy(chain, k, way).wait_recv()

    def rz_step(chain, k, way):
        j = half - k if way == 0 else half + k
        rz_arrived(chain, k - 1, way)
        for lo in range(0, hb, ROWS):
            rows = pl.ds(lo, ROWS)
            total = summed(j, chain, lo)
            for s in range(4):
                value = total[s] + zin[way, k - 1, chain, s, rows, :].astype(jnp.float32)
                zout[way, k, chain, s, rows, :] = value.astype(jnp.bfloat16)
        rz_copy(chain, k, way).start()

    def rz_final(chain, lo):
        rows = pl.ds(lo, ROWS)
        return [
            t + zin[0, half - 1, chain, s, rows, :].astype(jnp.float32)
            + zin[1, half - 1, chain, s, rows, :].astype(jnp.float32)
            for s, t in enumerate(summed(0, chain, lo))
        ]

    for chain in range(3):
        for s in range(2):
            zin[0, 0, chain, 2 + s] = jnp.zeros((hb, ob), jnp.bfloat16)
            zin[1, 0, chain, s] = jnp.zeros((hb, ob), jnp.bfloat16)
    give(half)
    rz_first(2)
    give(half - 1)
    give(half + 1)
    pass_on(half)
    rz_first(0)
    give(half - 2)
    give(half + 2)
    for way in range(2):
        rz_step(2, 1, way)
    pass_on(half - 1)
    pass_on(half + 1)
    arrived(half)
    rz_first(1)
    far_sum_copy = remote(far_out, far_in, want_sem, (4,), x2)

    def reduce_step(k, carry):
        @pl.when(k < half - 2)
        def _():
            give(half - k - 2)
            give(half + k + 2)

        @pl.when(k == half - 2)
        def _():
            give(0)

        for way in range(2):
            rz_step(0, k, way)

        @pl.when(k < half - 1)
        def _():
            for way in range(2):
                rz_step(2, k + 1, way)
            pass_on(half - k - 1)
            pass_on(half + k + 1)

        @pl.when(k == half - 1)
        def _():
            for way in range(2):
                rz_arrived(2, half - 1, way)
            for lo in range(0, hb, ROWS):
                for s, value in enumerate(rz_final(2, lo)):
                    far_out[s, pl.ds(lo, ROWS), :] = value.astype(jnp.bfloat16)
            far_sum_copy.start()
            pass_on(0)

        for way in range(2):
            arrived(half - k if way == 0 else half + k)
            rz_step(1, k, way)
        return carry

    lax.fori_loop(1, half, reduce_step, 0)

    for d in range(1, cols):
        lnv_copy(d).wait_recv()

    def left_step(n, carry):
        for t in range(8):
            lnv_cat[n, :, pl.ds(ob * t, ob)] = lnv_all[left_at[8 * n + t]]
        return carry

    lax.fori_loop(0, 4, left_step, 0)
    arrived(0)
    for way in range(2):
        rz_arrived(0, half - 1, way)
        rz_arrived(1, half - 1, way)
    far_sum_copy.wait_recv()
    for chain in range(2):
        for lo in range(0, hb, ROWS):
            rows = pl.ds(hb * chain + lo, ROWS)
            for s, value in enumerate(rz_final(chain, lo)):
                if chain == 0:
                    value = value + far_in[s, pl.ds(lo, ROWS), :].astype(jnp.float32)
                ham_out[s, rows, :] = value
                ham_half[s, rows, :] = value.astype(jnp.bfloat16)

    def reduce_sent():
        def sent_x(j, carry):
            for way in range(2):
                rx_copy(j, way).wait_send()
                rf_copy(j, way).wait_send()
            return carry

        def sent_z(k, carry):
            for chain in range(3):
                for way in range(2):
                    rz_copy(chain, k, way).wait_send()
            return carry

        for chain in range(3):
            for way in range(2):
                rz_copy(chain, 0, way, 2 * way, 2 * way + 2).wait_send()
        far_sum_copy.wait_send()
        lax.fori_loop(0, depth, sent_x, 0)
        lax.fori_loop(1, half, sent_z, 0)

    def win_copy(src, dst, first, n):
        return remote(src, dst.at[pl.ds(8 * n, 4)], win_sem, (first + n,), (wp, wm)[n])

    def product(n, win):
        chosen = jnp.concatenate([win[right_at[8 * n + t]] for t in range(8)], axis=0)
        return jnp.dot(lnv_cat[n], chosen, preferred_element_type=jnp.float32)

    for n in range(2):
        win_copy(ham_half, window, 0, n).start()
    for s in range(4):
        window[4 + s] = ham_half[s]
    for n in range(2):
        win_copy(ham_half, window, 0, n).wait_recv()
    for n in range(4):
        first = product(n, window)
        grad_out[n] = first
        first_half[n] = first.astype(jnp.bfloat16)
    for n in range(2):
        win_copy(first_half, window2, 2, n).start()
    for s in range(4):
        window2[4 + s] = first_half[s]
    for n in range(2):
        win_copy(first_half, window2, 2, n).wait_recv()
    for n in range(4):
        grad_out[n] = 3.0 * grad_out[n] - 2.0 * product(n, window2)

    gather_sent()
    halo_sent()
    reduce_sent()
    for n in range(2):
        win_copy(ham_half, window, 0, n).wait_send()
        win_copy(first_half, window2, 2, n).wait_send()


def body(phi_values, density, lnv_matrix, core_density, pair_owner, pair_source, term_left, term_right):
    phi = phi_values[0, 0]
    tiles, _, points = phi.shape
    ob = density.shape[-1]
    depth = lax.axis_size("wide") // NX
    cols = lax.axis_size("col")
    half = depth // 2
    slot_pair, slot_source, entry = place_arrays(pair_owner[0, 0, :, 0], pair_source[0, 0], depth)
    req = jnp.broadcast_to(slot_source[:, None], (2 * NX * depth, ob))
    row = jnp.arange(2, dtype=jnp.int32)[:, None, None]
    left_at = jnp.mod(term_left // 2 - lax.axis_index("col"), cols) * 4 + row * 2 + term_left % 2
    slabs, strips, deep = core_density.shape
    core = (
        core_density.reshape(slabs, strips, tiles, deep // tiles).transpose(2, 0, 1, 3).reshape(tiles, points)
    )
    block = lambda *n: pltpu.VMEM((*n, ob, ob), jnp.bfloat16)
    halves = lambda *n: pltpu.VMEM((*n, ob // 2, ob), jnp.bfloat16)
    sems = lambda *n: pltpu.SemaphoreType.DMA((2, *n))
    vmem = pl.BlockSpec(memory_space=pltpu.VMEM)
    smem = pl.BlockSpec(memory_space=pltpu.SMEM)
    pot, ham, grad = pl.pallas_call(
        functools.partial(step_kernel, depth),
        out_shape=(
            jax.ShapeDtypeStruct((tiles, points), jnp.float32),
            jax.ShapeDtypeStruct((4, ob, ob), jnp.float32),
            jax.ShapeDtypeStruct((4, ob, ob), jnp.float32),
        ),
        in_specs=[smem] * 4 + [vmem] * 4 + [pl.BlockSpec(memory_space=pl.ANY)],
        out_specs=(vmem, vmem, vmem),
        scratch_shapes=[
            pltpu.VMEM(phi.shape, jnp.bfloat16),
            pltpu.VMEM(req.shape, jnp.int32),
            halves(24 * depth),
            halves(2, depth, 5),
            block(9 * tiles + 1),
            halves(2, depth, 5),
            halves(depth, 5),
            halves(depth, 5),
            halves(depth),
            halves(depth),
            halves(2, half, 3, 4),
            halves(2, half, 3, 4),
            halves(4),
            halves(4),
            block(4 * cols),
            pltpu.VMEM((4, ob, 8 * ob), jnp.bfloat16),
            pltpu.VMEM((3 * ob, 3 * ob), jnp.bfloat16),
            pltpu.VMEM((tiles, points), jnp.float32),
            pltpu.VMEM((4, tiles, points), jnp.float32),
            pltpu.VMEM((2, tiles, points), jnp.float32),
            pltpu.VMEM((4, tiles, points), jnp.float32),
            block(12),
            block(12),
            block(4),
            block(4),
            pltpu.SemaphoreType.DMA,
            sems(5),
            sems(cols),
            sems(3, 2, half),
            sems(2, depth),
            sems(2, depth),
            sems(2, depth),
            sems(2, depth),
            sems(3, 2, half),
            sems(8),
            sems(4),
        ],
        compiler_params=pltpu.CompilerParams(
            collective_id=0, has_side_effects=True, vmem_limit_bytes=48 * 1024 * 1024
        ),
    )(
        slot_pair,
        entry,
        left_at.reshape(-1),
        term_right.reshape(-1),
        req,
        density.reshape(8, ob // 2, ob),
        lnv_matrix.reshape(4, ob, ob),
        core,
        phi,
    )
    potential = (
        pot.reshape(tiles, slabs, strips, deep // tiles).transpose(1, 2, 0, 3).reshape(slabs, strips, deep)
    )
    return potential, ham.reshape(density.shape), grad.reshape(density.shape)


def solution(mesh):
    grid = lambda n: P("wide", "col", *([None] * n))
    return jax.shard_map(
        body,
        mesh=mesh,
        in_specs=(grid(3), grid(2), grid(2), grid(1), grid(2), grid(1), grid(1), grid(1)),
        out_specs=(grid(1), grid(2), grid(2)),
        check_vma=False,
    )
```

```python
import functools
import math

import jax
import jax.numpy as jnp
from jax import lax
from jax.experimental import pallas as pl
from jax.experimental.pallas import tpu as pltpu
from jax.sharding import PartitionSpec as P

MESH = pl.DeviceIdType.MESH
NX = 4
SPACING = 0.1
KAPPA = 0.804
MU = 0.2195
FERMI_SQ = (3.0 * math.pi**2) ** (2.0 / 3.0)
AMPLITUDE = 0.75 * (3.0 / math.pi) ** (1.0 / 3.0)
VMEM_BYTES = 63 * 2**20
ROWS = 32


def pair_places(owner, source, z, x, depth):
    pairs = owner.shape[1]
    slots = 2 * NX * depth
    row = lax.broadcasted_iota(jnp.int32, (pairs, pairs), 0)
    lane = lax.broadcasted_iota(jnp.int32, (pairs, pairs), 1)
    along = owner
    down = jnp.sum(jnp.where(row == lane, along, 0), axis=1, keepdims=True)
    seat = jnp.sum(jnp.where((down == along) & (row < lane), 1, 0), axis=0, keepdims=True)
    seat = jnp.minimum(seat, 1)
    dz = lax.shift_right_logical(along, 2) - z
    dz = jnp.where(dz < 0, dz + depth, dz)
    dx = (along & 3) - x
    dx = jnp.where(dx < 0, dx + NX, dx)
    slot = dx * (2 * depth) + dz * 2 + seat
    hit = slot == lax.broadcasted_iota(jnp.int32, (slots, pairs), 0)
    slot_source = jnp.sum(jnp.where(hit, source + 1, 0), axis=1, keepdims=True) - 1
    slot_down = jnp.sum(jnp.where(row == lane, slot, 0), axis=1, keepdims=True)
    place = lax.broadcasted_iota(jnp.int32, (pairs, 128), 0)
    hit = slot_down == lax.broadcasted_iota(jnp.int32, (pairs, 128), 1)
    slot_pair = jnp.min(jnp.where(hit, place, pairs), axis=0, keepdims=True)
    halves = []
    for part in range(2):
        near = dz * 5 + seat * 2 + part
        far = 18 * depth + seat * depth + dz if part else 20 * depth + dz * 4 + source
        halves.append(
            jnp.where(
                dx == 0,
                dz * 8 + part * 4 + source,
                jnp.where(dx == 3, 8 * depth + near, jnp.where(dx == 1, 13 * depth + near, far)),
            )
        )
    return slot_source, slot_pair, halves


def step_kernel(
    depth,
    term_left,
    term_right,
    owner_hbm,
    source_hbm,
    dens_hbm,
    lnv_hbm,
    core_hbm,
    phi_hbm,
    pot_hbm,
    ham_hbm,
    grad_hbm,
    pot_out,
    ham_out,
    grad_out,
    owner,
    source,
    core_field,
    core,
    phi,
    places,
    index,
    req,
    want,
    buf,
    xsend,
    parts,
    rsend,
    rleft,
    rright,
    rfleft,
    rfright,
    zin,
    zout,
    far_in,
    far_out,
    lnv_all,
    lnv_cat,
    tile_matrix,
    charge,
    halo,
    flux,
    halo2,
    pot,
    window,
    window2,
    ham_half,
    first_half,
    load_sem,
    want_sem,
    lnv_sem,
    z_sem,
    x_sem,
    f_sem,
    rx_sem,
    rf_sem,
    rz_sem,
    halo_sem,
    win_sem,
    out_sem,
):
    w = lax.axis_index("wide")
    c = lax.axis_index("col")
    wides = depth * NX
    cols = lax.axis_size("col")
    tiles = charge.shape[0]
    half = depth // 2
    ob = phi.shape[1] // 3
    hb = ob // 2
    z, x = lax.div(w, NX), lax.rem(w, NX)

    def chip(dz, dx):
        return (lax.rem(z + depth + dz, depth) * NX + lax.rem(x + NX + dx, NX), c)

    slots = 2 * NX * depth
    zup, zdn, xr, xl, x2 = chip(1, 0), chip(-1, 0), chip(0, 1), chip(0, -1), chip(0, 2)
    wp = (lax.rem(w + 1, wides), c)
    wm = (lax.rem(w + wides - 1, wides), c)
    cp, cm = (w, lax.rem(c + 1, cols)), (w, lax.rem(c + cols - 1, cols))

    def remote(src, dst, sems, index, device):
        return pltpu.make_async_remote_copy(
            src_ref=src,
            dst_ref=dst,
            send_sem=sems.at[(0, *index)],
            recv_sem=sems.at[(1, *index)],
            device_id=device,
            device_id_type=MESH,
        )

    barrier = pltpu.get_barrier_semaphore()
    greeted = [zup, zdn, xr, xl, x2, wp, wm, cp, cm]
    for device in greeted:
        pl.semaphore_signal(barrier, inc=1, device_id=device, device_id_type=MESH)

    loads = [
        pltpu.make_async_copy(src, dst, load_sem.at[n])
        for n, (src, dst) in enumerate(
            (
                (owner_hbm, owner),
                (source_hbm, source),
                (dens_hbm.at[:, 0], buf.at[pl.ds(0, 4)]),
                (dens_hbm.at[:, 1], buf.at[pl.ds(4, 4)]),
                (lnv_hbm, lnv_all.at[pl.ds(0, 4)]),
                (core_hbm, core_field),
                (phi_hbm, phi),
            )
        )
    ]
    for load in loads:
        load.start()
    loads[0].wait()
    loads[1].wait()
    slot_source, slot_pair_row, halves = pair_places(owner[...], source[...], z, x, depth)
    req[...] = jnp.broadcast_to(slot_source, req.shape)
    want[pl.ds(0, 2 * depth), :] = req[pl.ds(0, 2 * depth), :]
    places[...] = jnp.zeros_like(places)
    places[pl.ds(0, 1), :] = slot_pair_row
    for part in range(2):
        places[pl.ds(1 + part, 1), pl.ds(0, 9 * tiles)] = halves[part]
    index_copy = pltpu.make_async_copy(places, index, load_sem.at[7])
    index_copy.start()

    def pair_of(dx, j, seat):
        return index[0, dx * span + 2 * j + seat]

    loads[2].wait()
    loads[3].wait()
    pl.semaphore_wait(barrier, len(greeted))

    left0, right0, fleft0, fright0, far0 = 8 * depth, 13 * depth, 18 * depth, 19 * depth, 20 * depth
    span = 2 * depth

    def z_copy(chain, k, way, lo=0, hi=4):
        stride, base = (8, 0) if chain == 0 else (8, 4) if chain == 1 else (4, far0)
        if way == 0:
            src, dst = lax.rem(depth - k, depth), depth - k - 1
        else:
            src, dst = k, k + 1
        return remote(
            buf.at[pl.ds(stride * src + base + lo, hi - lo)],
            buf.at[pl.ds(stride * dst + base + lo, hi - lo)],
            z_sem, (chain, way, k), (zup, zdn)[way],
        )

    def z_first(chain):
        for way in range(2):
            z_copy(chain, 0, way).start()

    def z_step(chain, k):
        for way in range(2):
            z_copy(chain, k - 1, way).wait_recv()
            z_copy(chain, k, way).start()

    def z_half(chain):
        for way in range(2):
            z_copy(chain, half - 2, way).wait_recv()
            z_copy(chain, half - 1, way, 2 * way, 2 * way + 2).start()

    def z_last(chain):
        for way in range(2):
            z_copy(chain, half - 1, way, 2 * way, 2 * way + 2).wait_recv()

    def x_copy(j, way):
        if way == 0:
            return remote(xsend.at[0, j], buf.at[pl.ds(left0 + 5 * j, 5)], x_sem, (0, j), xr)
        return remote(xsend.at[1, j], buf.at[pl.ds(right0 + 5 * j, 5)], x_sem, (1, j), xl)

    def f_copy(j, way):
        if way == 0:
            return remote(buf.at[left0 + 5 * j + 4], buf.at[fleft0 + j], f_sem, (0, j), xr)
        return remote(buf.at[right0 + 5 * j + 4], buf.at[fright0 + j], f_sem, (1, j), xl)

    def pack(j):
        wanted = (((3, 0), (3, 1), (2, 0)), ((1, 0), (1, 1), (2, 1)))
        for h in range(2):
            for lo in range(0, hb, ROWS):
                rows = pl.ds(lo, ROWS)
                b = [buf[8 * j + 4 * h + s, rows, :].astype(jnp.float32) for s in range(4)]
                for way in range(2):
                    for n, (dx, seat) in enumerate(wanted[way]):
                        if n == 2 and h == 0:
                            continue
                        src = want[pl.ds(dx * span + 2 * j + seat, 1), :]
                        got = jnp.where(
                            src == 0, b[0], jnp.where(src == 1, b[1], jnp.where(src == 2, b[2], b[3]))
                        )
                        xsend[way, j, 4 if n == 2 else 2 * n + h, rows, :] = got.astype(jnp.bfloat16)
        for way in range(2):
            x_copy(j, way).start()

    def forward(j):
        for way in range(2):
            x_copy(j, way).wait_recv()
            f_copy(j, way).start()

    def want_copy(dx, device):
        rows = pl.ds(dx * span, span)
        return remote(req.at[rows], want.at[rows], want_sem, (dx,), device)

    want_copies = [want_copy(1, xr), want_copy(3, xl), want_copy(2, x2)]
    for copy in want_copies:
        copy.start()
    far_copy = remote(buf.at[pl.ds(0, 4)], buf.at[pl.ds(far0, 4)], want_sem, (0,), x2)
    far_copy.start()
    z_first(0)
    z_first(1)

    turn = cols // 2

    def lnv_copy(k, way):
        lo, n = (2 * way, 2) if k == turn - 1 else (0, 4)
        src, dst = ((cols - k) % cols, cols - k - 1) if way == 0 else (k, k + 1)
        return remote(
            lnv_all.at[pl.ds(4 * src + lo, n)], lnv_all.at[pl.ds(4 * dst + lo, n)], lnv_sem, (way, k), (cp, cm)[way]
        )

    loads[4].wait()
    for way in range(2):
        lnv_copy(0, way).start()
    for copy in want_copies:
        copy.wait_recv()
    pack(0)
    far_copy.wait_recv()
    z_first(2)

    def gather_step(k, carry):
        z_step(0, k)
        z_step(1, k)
        pack(depth - k)
        pack(k)
        z_step(2, k)
        for n in range(1, turn):

            @pl.when(k == n + 1)
            def _():
                for way in range(2):
                    lnv_copy(n - 1, way).wait_recv()
                    lnv_copy(n, way).start()

        @pl.when(k == 2)
        def _():
            forward(0)

        @pl.when(k > 2)
        def _():
            forward(depth - k + 2)
            forward(k - 2)

        return carry

    lax.fori_loop(1, half - 1, gather_step, 0)
    z_half(0)
    z_half(1)
    pack(half + 1)
    pack(half - 1)
    z_half(2)
    for k in range(half - 3, half - 1):
        if k == 0:
            forward(0)
        elif k > 0:
            forward(depth - k)
            forward(k)
    z_last(0)
    z_last(1)
    pack(half)
    forward(half + 1)
    forward(half - 1)
    forward(half)
    z_last(2)

    def gather_end(j, carry):
        for way in range(2):
            f_copy(j, way).wait_recv()
        return carry

    loads[5].wait()
    field = core_field[...]
    if field.shape[1] < 128:
        field = jnp.pad(field, ((0, 0), (0, 128 - field.shape[1])))
    group = lax.div(lax.broadcasted_iota(jnp.int32, (32, 128), 1), 16)
    own_group = group[:8] == lax.broadcasted_iota(jnp.int32, (8, 128), 0)

    def spread(a):
        for shift in (64, 32, 16):
            a = a + pltpu.roll(a, shift, 1)
        return a

    for t in range(tiles):
        every = spread(jnp.where(group == t, field, 0.0))
        for n in range(4):
            chosen = jnp.where(own_group, every[8 * n : 8 * n + 8], 0.0)
            core[pl.ds(t, 1), pl.ds(128 * n, 128)] = jnp.sum(chosen, axis=0, keepdims=True)
    lax.fori_loop(0, depth, gather_end, 0)
    loads[6].wait()
    index_copy.wait()

    def gather_sent():
        def sent_x(j, carry):
            for way in range(2):
                x_copy(j, way).wait_send()
                f_copy(j, way).wait_send()
            return carry

        def sent_z(k, carry):
            for chain in range(3):
                for way in range(2):
                    z_copy(chain, k, way).wait_send()
            return carry

        for copy in want_copies:
            copy.wait_send()
        far_copy.wait_send()
        for k in range(turn):
            for way in range(2):
                lnv_copy(k, way).wait_send()
        for chain in range(3):
            for way in range(2):
                z_copy(chain, half - 1, way, 2 * way, 2 * way + 2).wait_send()
        lax.fori_loop(0, depth, sent_x, 0)
        lax.fori_loop(0, half - 1, sent_z, 0)


    def charge_step(t, carry):
        for a in range(3):
            for b in range(3):
                for h in range(2):
                    tile_matrix[pl.ds(ob * a + hb * h, hb), pl.ds(ob * b, ob)] = buf[
                        index[1 + h, 9 * t + 3 * a + b]
                    ]
        values = phi[t]
        applied = jnp.dot(tile_matrix[...], values, preferred_element_type=jnp.float32)
        charge[pl.ds(t, 1), :] = jnp.sum(values.astype(jnp.float32) * applied, axis=0, keepdims=True)
        return carry

    lax.fori_loop(0, tiles, charge_step, 0, unroll=2)

    sides = (wp, wm, cp, cm)

    def halo_copy(src, dst, first, n):
        return remote(src, dst.at[n], halo_sem, (first + n,), sides[n])

    for n in range(4):
        halo_copy(charge, halo, 0, n).start()

    points = charge.shape[1]
    xcell, ycell, zcell = points // 2, points // 32, 1
    lane = lax.broadcasted_iota(jnp.int32, (tiles, points), 1)
    at_x = lax.div(lane, xcell)
    at_y = lax.rem(lax.div(lane, ycell), 16)
    at_z = lax.rem(lane, 16)

    def turned(a, shift):
        return pltpu.roll(a, shift % points, 1)

    def x_next(a, beyond):
        return turned(jnp.where(at_x == 1, a, beyond), xcell)

    def x_prev(a, beyond):
        return turned(jnp.where(at_x == 0, a, beyond), xcell)

    def y_next(a, beyond):
        return jnp.where(at_y < 15, turned(a, -ycell), turned(beyond, 15 * ycell))

    def y_prev(a, beyond):
        return jnp.where(at_y > 0, turned(a, ycell), turned(beyond, -15 * ycell))

    def z_next(a):
        return jnp.where(at_z < 15, turned(a, -1), turned(pltpu.roll(a, tiles - 1, 0), 15))

    def z_prev(a):
        return jnp.where(at_z > 0, turned(a, 1), turned(pltpu.roll(a, 1, 0), -15))

    rho = charge[...]
    for n in range(4):
        halo_copy(charge, halo, 0, n).wait_recv()
    grad_x = (x_next(rho, halo[1]) - x_prev(rho, halo[0])) / (2.0 * SPACING)
    grad_y = (y_next(rho, halo[3]) - y_prev(rho, halo[2])) / (2.0 * SPACING)
    grad_z = (z_next(rho) - z_prev(rho)) / (2.0 * SPACING)
    sigma = grad_x * grad_x + grad_y * grad_y + grad_z * grad_z
    n_sq = rho * rho + core[...] * core[...]
    third = jnp.exp(jnp.log(n_sq) * (1.0 / 6.0))
    smooth = jnp.sqrt(n_sq)
    four_thirds = smooth * third
    s2 = sigma / (4.0 * FERMI_SQ * four_thirds * four_thirds)
    denom = 1.0 + MU * s2 / KAPPA
    enhance = 1.0 + KAPPA - KAPPA / denom
    slope = MU / (denom * denom)
    de_dn = -AMPLITUDE * third * ((4.0 / 3.0) * enhance - (8.0 / 3.0) * s2 * slope)
    de_dsigma = -AMPLITUDE * slope / (4.0 * FERMI_SQ * four_thirds)
    flux_x = 2.0 * de_dsigma * grad_x
    flux_y = 2.0 * de_dsigma * grad_y
    flux_z = 2.0 * de_dsigma * grad_z
    flux[0] = flux_x
    flux[1] = flux_y
    for n in range(4):
        halo_copy(flux.at[n // 2], halo2, 4, n).start()
    partial = de_dn * rho / smooth + (z_prev(flux_z) - z_next(flux_z)) / (2.0 * SPACING)
    for n in range(4):
        halo_copy(flux.at[n // 2], halo2, 4, n).wait_recv()
    divergence = (
        x_prev(flux_x, halo2[0])
        - x_next(flux_x, halo2[1])
        + y_prev(flux_y, halo2[2])
        - y_next(flux_y, halo2[3])
    )
    pot[...] = partial + divergence / (2.0 * SPACING)

    def halo_sent():
        for n in range(4):
            halo_copy(charge, halo, 0, n).wait_send()
            halo_copy(flux.at[n // 2], halo2, 4, n).wait_send()

    parts[9 * tiles] = jnp.zeros((ob, ob), jnp.bfloat16)

    def part_step(t, carry):
        values = phi[t]
        weighted = (values.astype(jnp.float32) * pot[pl.ds(t, 1), :]).astype(jnp.bfloat16)
        block = lax.dot_general(
            weighted, values, (((1,), (1,)), ((), ())), preferred_element_type=jnp.float32
        ).astype(jnp.bfloat16)
        for a in range(3):
            for b in range(3):
                parts[9 * t + 3 * a + b] = block[ob * a : ob * a + ob, ob * b : ob * b + ob]
        return carry

    lax.fori_loop(0, tiles, part_step, 0, unroll=2)

    def rx_copy(j, way):
        return remote(rsend.at[way, j], (rleft, rright)[way].at[j], rx_sem, (way, j), (xr, xl)[way])

    def rf_copy(j, way):
        return remote(
            (rleft, rright)[way].at[j, 4], (rfleft, rfright)[way].at[j], rf_sem, (way, j), (xr, xl)[way]
        )

    def rz_copy(chain, k, way, lo=0, hi=4):
        rows = pl.ds(lo, hi - lo)
        return remote(
            zout.at[way, k, chain, rows], zin.at[way, k, chain, rows], rz_sem, (chain, way, k), (zup, zdn)[way]
        )

    def give(j):
        slots = (((1, 0), (1, 1), (2, 0)), ((3, 0), (3, 1), (2, 1)))
        for way in range(2):
            for n, (dx, seat) in enumerate(slots[way]):
                pair = pair_of(dx, j, seat)
                if n < 2:
                    rsend[way, j, 2 * n] = parts[pair, :hb, :]
                    rsend[way, j, 2 * n + 1] = parts[pair, hb:, :]
                else:
                    rsend[way, j, 4] = parts[pair, hb:, :]
            rx_copy(j, way).start()

    def pass_on(j):
        for way in range(2):
            rx_copy(j, way).wait_recv()
            rf_copy(j, way).start()

    def by_source(pieces, j):
        total = [jnp.zeros((ROWS, ob), jnp.float32)] * 4
        for ref, dx, seat, piece in pieces:
            src = ref[pl.ds(dx * span + 2 * j + seat, 1), :]
            piece = piece.astype(jnp.float32)
            total = [t + jnp.where(src == s, piece, 0.0) for s, t in enumerate(total)]
        return total

    def summed(j, chain, lo):
        rows = pl.ds(lo, ROWS)
        if chain == 2:
            return by_source(
                [(req, 2, s, parts[pair_of(2, j, s), rows, :]) for s in range(2)], j
            )
        pieces = [
            (req, 0, s, parts[pair_of(0, j, s), pl.ds(hb * chain + lo, ROWS), :]) for s in range(2)
        ]
        for s in range(2):
            pieces.append((want, 1, s, rleft[j, 2 * s + chain, rows, :]))
            pieces.append((want, 3, s, rright[j, 2 * s + chain, rows, :]))
        if chain == 1:
            pieces.append((want, 2, 0, rfleft[j, rows, :]))
            pieces.append((want, 2, 1, rfright[j, rows, :]))
        return by_source(pieces, j)

    def arrived(j):
        for way in range(2):
            rf_copy(j, way).wait_recv()

    def rz_first(chain):
        for lo in range(0, hb, ROWS):
            total = summed(half, chain, lo)
            for s in range(4):
                zout[s // 2, 0, chain, s, pl.ds(lo, ROWS), :] = total[s].astype(jnp.bfloat16)
        for way in range(2):
            rz_copy(chain, 0, way, 2 * way, 2 * way + 2).start()

    def rz_arrived(chain, k, way):
        @pl.when(k == 0)
        def _():
            rz_copy(chain, 0, way, 2 * way, 2 * way + 2).wait_recv()

        @pl.when(k > 0)
        def _():
            rz_copy(chain, k, way).wait_recv()

    def rz_step(chain, k, way):
        j = half - k if way == 0 else half + k
        rz_arrived(chain, k - 1, way)
        for lo in range(0, hb, ROWS):
            rows = pl.ds(lo, ROWS)
            total = summed(j, chain, lo)
            for s in range(4):
                value = total[s] + zin[way, k - 1, chain, s, rows, :].astype(jnp.float32)
                zout[way, k, chain, s, rows, :] = value.astype(jnp.bfloat16)
        rz_copy(chain, k, way).start()

    def rz_final(chain, lo):
        rows = pl.ds(lo, ROWS)
        return [
            t + zin[0, half - 1, chain, s, rows, :].astype(jnp.float32)
            + zin[1, half - 1, chain, s, rows, :].astype(jnp.float32)
            for s, t in enumerate(summed(0, chain, lo))
        ]

    for chain in range(3):
        for s in range(2):
            zin[0, 0, chain, 2 + s] = jnp.zeros((hb, ob), jnp.bfloat16)
            zin[1, 0, chain, s] = jnp.zeros((hb, ob), jnp.bfloat16)
    give(half)
    rz_first(2)
    give(half - 1)
    give(half + 1)
    pass_on(half)
    rz_first(0)
    give(half - 2)
    give(half + 2)
    for way in range(2):
        rz_step(2, 1, way)
    pass_on(half - 1)
    pass_on(half + 1)
    arrived(half)
    rz_first(1)
    far_sum_copy = remote(far_out, far_in, want_sem, (4,), x2)

    def reduce_step(k, carry):
        @pl.when(k < half - 2)
        def _():
            give(half - k - 2)
            give(half + k + 2)

        @pl.when(k == half - 2)
        def _():
            give(0)

        for way in range(2):
            rz_step(0, k, way)

        @pl.when(k < half - 1)
        def _():
            for way in range(2):
                rz_step(2, k + 1, way)
            pass_on(half - k - 1)
            pass_on(half + k + 1)

        @pl.when(k == half - 1)
        def _():
            for way in range(2):
                rz_arrived(2, half - 1, way)
            for lo in range(0, hb, ROWS):
                for s, value in enumerate(rz_final(2, lo)):
                    far_out[s, pl.ds(lo, ROWS), :] = value.astype(jnp.bfloat16)
            far_sum_copy.start()
            pass_on(0)

        for way in range(2):
            arrived(half - k if way == 0 else half + k)
            rz_step(1, k, way)
        return carry

    lax.fori_loop(1, half, reduce_step, 0)

    for way in range(2):
        lnv_copy(turn - 1, way).wait_recv()
    for n in range(4):
        slab = jnp.zeros((8, 128), jnp.float32)
        for t in range(tiles):
            points_t = jnp.broadcast_to(pot[pl.ds(t, 1), pl.ds(128 * n, 128)], (8, 128))
            slab = jnp.where(group[:8] == t, spread(jnp.where(own_group, points_t, 0.0)), slab)
        pot_out[pl.ds(8 * n, 8), :] = slab[:, : 16 * tiles]

    pot_save = pltpu.make_async_copy(pot_out, pot_hbm, out_sem.at[0])
    pot_save.start()

    def left_step(n, carry):
        for t in range(8):
            slot = term_left[lax.div(n, 2), lax.rem(n, 2), t]
            column = lax.rem(lax.shift_right_logical(slot, 1) + cols - c, cols)
            lnv_cat[n, :, pl.ds(ob * t, ob)] = lnv_all[column * 4 + lax.div(n, 2) * 2 + (slot & 1)]
        return carry

    lax.fori_loop(0, 4, left_step, 0)
    arrived(0)
    for way in range(2):
        rz_arrived(0, half - 1, way)
        rz_arrived(1, half - 1, way)
    far_sum_copy.wait_recv()
    for chain in range(2):
        for lo in range(0, hb, ROWS):
            rows = pl.ds(hb * chain + lo, ROWS)
            for s, value in enumerate(rz_final(chain, lo)):
                if chain == 0:
                    value = value + far_in[s, pl.ds(lo, ROWS), :].astype(jnp.float32)
                ham_out[s, rows, :] = value
                ham_half[s, rows, :] = value.astype(jnp.bfloat16)

    def reduce_sent():
        def sent_x(j, carry):
            for way in range(2):
                rx_copy(j, way).wait_send()
                rf_copy(j, way).wait_send()
            return carry

        def sent_z(k, carry):
            for chain in range(3):
                for way in range(2):
                    rz_copy(chain, k, way).wait_send()
            return carry

        for chain in range(3):
            for way in range(2):
                rz_copy(chain, 0, way, 2 * way, 2 * way + 2).wait_send()
        far_sum_copy.wait_send()
        lax.fori_loop(0, depth, sent_x, 0)
        lax.fori_loop(1, half, sent_z, 0)

    def win_copy(src, dst, first, n):
        return remote(src, dst.at[pl.ds(8 * n, 4)], win_sem, (first + n,), (wp, wm)[n])

    def win_block(s, n):
        return remote(first_half.at[s], window2.at[8 * n + s], win_sem, (2 + 2 * s + n,), (wp, wm)[n])

    def product(n, win):
        chosen = jnp.concatenate([win[term_right[n // 2, n % 2, t]] for t in range(8)], axis=0)
        return jnp.dot(lnv_cat[n], chosen, preferred_element_type=jnp.float32)

    for n in range(2):
        win_copy(ham_half, window, 0, n).start()
    ham_save = pltpu.make_async_copy(ham_out, ham_hbm, out_sem.at[1])
    ham_save.start()
    for s in range(4):
        window[4 + s] = ham_half[s]
    for n in range(2):
        win_copy(ham_half, window, 0, n).wait_recv()
    for s in range(4):
        first = product(s, window)
        grad_out[s] = first
        first_half[s] = first.astype(jnp.bfloat16)
        for n in range(2):
            win_block(s, n).start()
    for s in range(4):
        window2[4 + s] = first_half[s]
    for s in range(4):
        for n in range(2):
            win_block(s, n).wait_recv()
    saves = [pot_save, ham_save]
    for s in range(4):
        grad_out[s] = 3.0 * grad_out[s] - 2.0 * product(s, window2)
        saves.append(pltpu.make_async_copy(grad_out.at[s], grad_hbm.at[s], out_sem.at[2 + s]))
        saves[-1].start()

    gather_sent()
    halo_sent()
    reduce_sent()
    for save in saves:
        save.wait()
    for n in range(2):
        win_copy(ham_half, window, 0, n).wait_send()
        for s in range(4):
            win_block(s, n).wait_send()


def save_kernel(*refs):
    sources, results, held, sems = refs[:3], refs[3:6], refs[6:9], refs[9]
    loads = [pltpu.make_async_copy(sources[n], held[n], sems.at[0, n]) for n in range(3)]
    saves = [pltpu.make_async_copy(held[n], results[n], sems.at[1, n]) for n in range(3)]
    for load in loads:
        load.start()
    for load, save in zip(loads, saves):
        load.wait()
        save.start()
    for save in saves:
        save.wait()


def body(phi_values, density, lnv_matrix, core_density, pair_owner, pair_source, term_left, term_right):
    phi = phi_values[0, 0]
    tiles, _, points = phi.shape
    ob = density.shape[-1]
    depth = lax.axis_size("wide") // NX
    cols = lax.axis_size("col")
    half = depth // 2
    slabs, strips, deep = core_density.shape
    slots = 2 * NX * depth
    shapes = tuple(
        jax.ShapeDtypeStruct(shape, jnp.float32) for shape in ((slabs * strips, deep), (4, ob, ob), (4, ob, ob))
    )
    block = lambda *n: pltpu.VMEM((*n, ob, ob), jnp.bfloat16)
    halves = lambda *n: pltpu.VMEM((*n, ob // 2, ob), jnp.bfloat16)
    sems = lambda *n: pltpu.SemaphoreType.DMA((2, *n))
    smem = pl.BlockSpec(memory_space=pltpu.SMEM)
    hbm = pl.BlockSpec(memory_space=pltpu.HBM)
    outs = pl.pallas_call(
        functools.partial(step_kernel, depth),
        out_shape=shapes,
        in_specs=[smem] * 2 + [hbm] * 6,
        out_specs=(hbm, hbm, hbm),
        scratch_shapes=[
            *[pltpu.VMEM(shape.shape, jnp.float32) for shape in shapes],
            pltpu.VMEM((1, 9 * tiles), jnp.int32),
            pltpu.VMEM((1, 9 * tiles), jnp.int32),
            pltpu.VMEM((slabs * strips, deep), jnp.float32),
            pltpu.VMEM((tiles, points), jnp.float32),
            pltpu.VMEM(phi.shape, jnp.bfloat16),
            pltpu.VMEM((8, 128), jnp.int32),
            pltpu.SMEM((8, 128), jnp.int32),
            pltpu.VMEM((slots, ob), jnp.int32),
            pltpu.VMEM((slots, ob), jnp.int32),
            halves(24 * depth),
            halves(2, depth, 5),
            block(9 * tiles + 1),
            halves(2, depth, 5),
            halves(depth, 5),
            halves(depth, 5),
            halves(depth),
            halves(depth),
            halves(2, half, 3, 4),
            halves(2, half, 3, 4),
            halves(4),
            halves(4),
            block(4 * cols),
            pltpu.VMEM((4, ob, 8 * ob), jnp.bfloat16),
            pltpu.VMEM((3 * ob, 3 * ob), jnp.bfloat16),
            pltpu.VMEM((tiles, points), jnp.float32),
            pltpu.VMEM((4, tiles, points), jnp.float32),
            pltpu.VMEM((2, tiles, points), jnp.float32),
            pltpu.VMEM((4, tiles, points), jnp.float32),
            pltpu.VMEM((tiles, points), jnp.float32),
            block(12),
            block(12),
            block(4),
            block(4),
            pltpu.SemaphoreType.DMA((8,)),
            sems(5),
            sems(2, cols // 2),
            sems(3, 2, half),
            sems(2, depth),
            sems(2, depth),
            sems(2, depth),
            sems(2, depth),
            sems(3, 2, half),
            sems(8),
            sems(10),
            pltpu.SemaphoreType.DMA((6,)),
        ],
        compiler_params=pltpu.CompilerParams(
            collective_id=0, has_side_effects=True, vmem_limit_bytes=VMEM_BYTES
        ),
    )(
        term_left,
        term_right,
        pair_owner.reshape(1, 9 * tiles),
        pair_source.reshape(1, 9 * tiles),
        density.reshape(4, 2, ob // 2, ob),
        lnv_matrix.reshape(4, ob, ob),
        core_density.reshape(slabs * strips, deep),
        phi,
    )
    pot, ham, grad = pl.pallas_call(
        save_kernel,
        out_shape=shapes,
        in_specs=[hbm] * 3,
        out_specs=(hbm, hbm, hbm),
        scratch_shapes=[*[pltpu.VMEM(shape.shape, jnp.float32) for shape in shapes], sems(3)],
    )(*outs)
    return pot.reshape(core_density.shape), ham.reshape(density.shape), grad.reshape(density.shape)


def solution(mesh):
    grid = lambda n: P("wide", "col", *([None] * n))
    return jax.shard_map(
        body,
        mesh=mesh,
        in_specs=(grid(3), grid(2), grid(2), grid(1), grid(2), grid(1), grid(1), grid(1)),
        out_specs=(grid(1), grid(2), grid(2)),
        check_vma=False,
    )
```

```python
import functools
import math

import jax
import jax.numpy as jnp
from jax import lax
from jax.experimental import pallas as pl
from jax.experimental.pallas import tpu as pltpu
from jax.sharding import PartitionSpec as P

MESH = pl.DeviceIdType.MESH
NX = 4
SPACING = 0.1
KAPPA = 0.804
MU = 0.2195
FERMI_SQ = (3.0 * math.pi**2) ** (2.0 / 3.0)
AMPLITUDE = 0.75 * (3.0 / math.pi) ** (1.0 / 3.0)
VMEM_BYTES = 63 * 2**20
ROWS = 32


def pair_places(owner, source, z, x, depth):
    pairs = owner.shape[1]
    slots = 2 * NX * depth
    row = lax.broadcasted_iota(jnp.int32, (pairs, pairs), 0)
    lane = lax.broadcasted_iota(jnp.int32, (pairs, pairs), 1)
    along = owner
    down = jnp.sum(jnp.where(row == lane, along, 0), axis=1, keepdims=True)
    seat = jnp.sum(jnp.where((down == along) & (row < lane), 1, 0), axis=0, keepdims=True)
    seat = jnp.minimum(seat, 1)
    dz = lax.shift_right_logical(along, 2) - z
    dz = jnp.where(dz < 0, dz + depth, dz)
    dx = (along & 3) - x
    dx = jnp.where(dx < 0, dx + NX, dx)
    slot = dx * (2 * depth) + dz * 2 + seat
    hit = slot == lax.broadcasted_iota(jnp.int32, (slots, pairs), 0)
    slot_source = jnp.sum(jnp.where(hit, source + 1, 0), axis=1, keepdims=True) - 1
    slot_down = jnp.sum(jnp.where(row == lane, slot, 0), axis=1, keepdims=True)
    place = lax.broadcasted_iota(jnp.int32, (pairs, 128), 0)
    hit = slot_down == lax.broadcasted_iota(jnp.int32, (pairs, 128), 1)
    slot_pair = jnp.min(jnp.where(hit, place, pairs), axis=0, keepdims=True)
    halves = []
    for part in range(2):
        near = dz * 5 + seat * 2 + part
        far = 18 * depth + seat * depth + dz if part else 20 * depth + dz * 4 + source
        halves.append(
            jnp.where(
                dx == 0,
                dz * 8 + part * 4 + source,
                jnp.where(dx == 3, 8 * depth + near, jnp.where(dx == 1, 13 * depth + near, far)),
            )
        )
    return slot_source, slot_pair, halves


def step_kernel(
    depth,
    term_left,
    term_right,
    owner_hbm,
    source_hbm,
    dens_hbm,
    lnv_hbm,
    core_hbm,
    phi_hbm,
    pot_hbm,
    ham_hbm,
    grad_hbm,
    pot_out,
    ham_out,
    grad_out,
    owner,
    source,
    core_field,
    core,
    phi,
    places,
    index,
    req,
    want,
    buf,
    xsend,
    parts,
    rsend,
    rleft,
    rright,
    rfleft,
    rfright,
    zin,
    zout,
    far_in,
    far_out,
    lnv_all,
    lnv_cat,
    tile_matrix,
    charge,
    halo,
    flux,
    halo2,
    pot,
    window,
    window2,
    ham_half,
    first_half,
    load_sem,
    want_sem,
    lnv_sem,
    z_sem,
    x_sem,
    f_sem,
    rx_sem,
    rf_sem,
    rz_sem,
    halo_sem,
    win_sem,
    out_sem,
):
    w = lax.axis_index("wide")
    c = lax.axis_index("col")
    wides = depth * NX
    cols = lax.axis_size("col")
    tiles = charge.shape[0]
    half = depth // 2
    ob = phi.shape[1] // 3
    hb = ob // 2
    z, x = lax.div(w, NX), lax.rem(w, NX)

    def chip(dz, dx):
        return (lax.rem(z + depth + dz, depth) * NX + lax.rem(x + NX + dx, NX), c)

    slots = 2 * NX * depth
    zup, zdn, xr, xl, x2 = chip(1, 0), chip(-1, 0), chip(0, 1), chip(0, -1), chip(0, 2)
    wp = (lax.rem(w + 1, wides), c)
    wm = (lax.rem(w + wides - 1, wides), c)
    cp, cm = (w, lax.rem(c + 1, cols)), (w, lax.rem(c + cols - 1, cols))

    def remote(src, dst, sems, index, device):
        return pltpu.make_async_remote_copy(
            src_ref=src,
            dst_ref=dst,
            send_sem=sems.at[(0, *index)],
            recv_sem=sems.at[(1, *index)],
            device_id=device,
            device_id_type=MESH,
        )

    barrier = pltpu.get_barrier_semaphore()
    greeted = [zup, zdn, xr, xl, x2, wp, wm, cp, cm]
    for device in greeted:
        pl.semaphore_signal(barrier, inc=1, device_id=device, device_id_type=MESH)

    loads = [
        pltpu.make_async_copy(src, dst, load_sem.at[n])
        for n, (src, dst) in enumerate(
            (
                (owner_hbm, owner),
                (source_hbm, source),
                (dens_hbm.at[:, 0], buf.at[pl.ds(0, 4)]),
                (dens_hbm.at[:, 1], buf.at[pl.ds(4, 4)]),
                (lnv_hbm, lnv_all.at[pl.ds(0, 4)]),
                (core_hbm, core_field),
                (phi_hbm, phi),
            )
        )
    ]
    for load in loads:
        load.start()
    loads[0].wait()
    loads[1].wait()
    slot_source, slot_pair_row, halves = pair_places(owner[...], source[...], z, x, depth)
    req[...] = jnp.broadcast_to(slot_source, req.shape)
    want[pl.ds(0, 2 * depth), :] = req[pl.ds(0, 2 * depth), :]
    places[...] = jnp.zeros_like(places)
    places[pl.ds(0, 1), :] = slot_pair_row
    for part in range(2):
        places[pl.ds(1 + part, 1), pl.ds(0, 9 * tiles)] = halves[part]
    index_copy = pltpu.make_async_copy(places, index, load_sem.at[7])
    index_copy.start()

    def pair_of(dx, j, seat):
        return index[0, dx * span + 2 * j + seat]

    loads[2].wait()
    loads[3].wait()
    pl.semaphore_wait(barrier, len(greeted))

    left0, right0, fleft0, fright0, far0 = 8 * depth, 13 * depth, 18 * depth, 19 * depth, 20 * depth
    span = 2 * depth

    def z_copy(chain, k, way, lo=0, hi=4):
        stride, base = (8, 0) if chain == 0 else (8, 4) if chain == 1 else (4, far0)
        if way == 0:
            src, dst = lax.rem(depth - k, depth), depth - k - 1
        else:
            src, dst = k, k + 1
        return remote(
            buf.at[pl.ds(stride * src + base + lo, hi - lo)],
            buf.at[pl.ds(stride * dst + base + lo, hi - lo)],
            z_sem, (chain, way, k), (zup, zdn)[way],
        )

    def z_first(chain):
        for way in range(2):
            z_copy(chain, 0, way).start()

    def z_step(chain, k):
        for way in range(2):
            z_copy(chain, k - 1, way).wait_recv()
            z_copy(chain, k, way).start()

    def z_half(chain):
        for way in range(2):
            z_copy(chain, half - 2, way).wait_recv()
            z_copy(chain, half - 1, way, 2 * way, 2 * way + 2).start()

    def z_last(chain):
        for way in range(2):
            z_copy(chain, half - 1, way, 2 * way, 2 * way + 2).wait_recv()

    def x_copy(j, way):
        if way == 0:
            return remote(xsend.at[0, j], buf.at[pl.ds(left0 + 5 * j, 5)], x_sem, (0, j), xr)
        return remote(xsend.at[1, j], buf.at[pl.ds(right0 + 5 * j, 5)], x_sem, (1, j), xl)

    def f_copy(j, way):
        if way == 0:
            return remote(buf.at[left0 + 5 * j + 4], buf.at[fleft0 + j], f_sem, (0, j), xr)
        return remote(buf.at[right0 + 5 * j + 4], buf.at[fright0 + j], f_sem, (1, j), xl)

    def pack(j):
        wanted = (((3, 0), (3, 1), (2, 0)), ((1, 0), (1, 1), (2, 1)))
        for h in range(2):
            for lo in range(0, hb, ROWS):
                rows = pl.ds(lo, ROWS)
                b = [buf[8 * j + 4 * h + s, rows, :].astype(jnp.float32) for s in range(4)]
                for way in range(2):
                    for n, (dx, seat) in enumerate(wanted[way]):
                        if n == 2 and h == 0:
                            continue
                        src = want[pl.ds(dx * span + 2 * j + seat, 1), :]
                        got = jnp.where(
                            src == 0, b[0], jnp.where(src == 1, b[1], jnp.where(src == 2, b[2], b[3]))
                        )
                        xsend[way, j, 4 if n == 2 else 2 * n + h, rows, :] = got.astype(jnp.bfloat16)
        for way in range(2):
            x_copy(j, way).start()

    def forward(j):
        for way in range(2):
            x_copy(j, way).wait_recv()
            f_copy(j, way).start()

    def want_copy(dx, device):
        rows = pl.ds(dx * span, span)
        return remote(req.at[rows], want.at[rows], want_sem, (dx,), device)

    want_copies = [want_copy(1, xr), want_copy(3, xl), want_copy(2, x2)]
    for copy in want_copies:
        copy.start()
    far_copy = remote(buf.at[pl.ds(0, 4)], buf.at[pl.ds(far0, 4)], want_sem, (0,), x2)
    far_copy.start()
    z_first(0)
    z_first(1)

    turn = cols // 2

    def lnv_copy(k, way):
        lo, n = (2 * way, 2) if k == turn - 1 else (0, 4)
        src, dst = ((cols - k) % cols, cols - k - 1) if way == 0 else (k, k + 1)
        return remote(
            lnv_all.at[pl.ds(4 * src + lo, n)], lnv_all.at[pl.ds(4 * dst + lo, n)], lnv_sem, (way, k), (cp, cm)[way]
        )

    loads[4].wait()
    for way in range(2):
        lnv_copy(0, way).start()
    for copy in want_copies:
        copy.wait_recv()
    pack(0)
    far_copy.wait_recv()
    z_first(2)

    def gather_step(k, carry):
        z_step(0, k)
        z_step(1, k)
        pack(depth - k)
        pack(k)
        z_step(2, k)
        for n in range(1, turn):

            @pl.when(k == n + 1)
            def _():
                for way in range(2):
                    lnv_copy(n - 1, way).wait_recv()
                    lnv_copy(n, way).start()

        @pl.when(k == 1)
        def _():
            forward(0)

        @pl.when(k > 1)
        def _():
            forward(depth - k + 1)
            forward(k - 1)

        return carry

    lax.fori_loop(1, half - 1, gather_step, 0)
    z_half(0)
    z_half(1)
    pack(half + 1)
    pack(half - 1)
    z_half(2)
    for k in range(half - 2, half - 1):
        if k == 0:
            forward(0)
        elif k > 0:
            forward(depth - k)
            forward(k)
    z_last(0)
    z_last(1)
    pack(half)
    forward(half + 1)
    forward(half - 1)
    forward(half)
    z_last(2)

    def gather_end(j, carry):
        for way in range(2):
            f_copy(j, way).wait_recv()
        return carry

    loads[5].wait()
    field = core_field[...]
    if field.shape[1] < 128:
        field = jnp.pad(field, ((0, 0), (0, 128 - field.shape[1])))
    group = lax.div(lax.broadcasted_iota(jnp.int32, (32, 128), 1), 16)
    own_group = group[:8] == lax.broadcasted_iota(jnp.int32, (8, 128), 0)

    def spread(a):
        for shift in (64, 32, 16):
            a = a + pltpu.roll(a, shift, 1)
        return a

    for t in range(tiles):
        every = spread(jnp.where(group == t, field, 0.0))
        for n in range(4):
            chosen = jnp.where(own_group, every[8 * n : 8 * n + 8], 0.0)
            core[pl.ds(t, 1), pl.ds(128 * n, 128)] = jnp.sum(chosen, axis=0, keepdims=True)
    lax.fori_loop(0, depth, gather_end, 0)
    loads[6].wait()
    index_copy.wait()

    def gather_sent():
        def sent_x(j, carry):
            for way in range(2):
                x_copy(j, way).wait_send()
                f_copy(j, way).wait_send()
            return carry

        def sent_z(k, carry):
            for chain in range(3):
                for way in range(2):
                    z_copy(chain, k, way).wait_send()
            return carry

        for copy in want_copies:
            copy.wait_send()
        far_copy.wait_send()
        for k in range(turn):
            for way in range(2):
                lnv_copy(k, way).wait_send()
        for chain in range(3):
            for way in range(2):
                z_copy(chain, half - 1, way, 2 * way, 2 * way + 2).wait_send()
        lax.fori_loop(0, depth, sent_x, 0)
        lax.fori_loop(0, half - 1, sent_z, 0)


    def charge_step(t, carry):
        for a in range(3):
            for b in range(3):
                for h in range(2):
                    tile_matrix[pl.ds(ob * a + hb * h, hb), pl.ds(ob * b, ob)] = buf[
                        index[1 + h, 9 * t + 3 * a + b]
                    ]
        values = phi[t]
        applied = jnp.dot(tile_matrix[...], values, preferred_element_type=jnp.float32)
        charge[pl.ds(t, 1), :] = jnp.sum(values.astype(jnp.float32) * applied, axis=0, keepdims=True)
        return carry

    lax.fori_loop(0, tiles, charge_step, 0, unroll=4)

    sides = (wp, wm, cp, cm)

    def halo_copy(src, dst, first, n):
        return remote(src, dst.at[n], halo_sem, (first + n,), sides[n])

    for n in range(4):
        halo_copy(charge, halo, 0, n).start()

    points = charge.shape[1]
    xcell, ycell, zcell = points // 2, points // 32, 1
    lane = lax.broadcasted_iota(jnp.int32, (tiles, points), 1)
    at_x = lax.div(lane, xcell)
    at_y = lax.rem(lax.div(lane, ycell), 16)
    at_z = lax.rem(lane, 16)

    def turned(a, shift):
        return pltpu.roll(a, shift % points, 1)

    def x_next(a, beyond):
        return turned(jnp.where(at_x == 1, a, beyond), xcell)

    def x_prev(a, beyond):
        return turned(jnp.where(at_x == 0, a, beyond), xcell)

    def y_next(a, beyond):
        return jnp.where(at_y < 15, turned(a, -ycell), turned(beyond, 15 * ycell))

    def y_prev(a, beyond):
        return jnp.where(at_y > 0, turned(a, ycell), turned(beyond, -15 * ycell))

    def z_next(a):
        return jnp.where(at_z < 15, turned(a, -1), turned(pltpu.roll(a, tiles - 1, 0), 15))

    def z_prev(a):
        return jnp.where(at_z > 0, turned(a, 1), turned(pltpu.roll(a, 1, 0), -15))

    rho = charge[...]
    for n in range(4):
        halo_copy(charge, halo, 0, n).wait_recv()
    grad_x = (x_next(rho, halo[1]) - x_prev(rho, halo[0])) / (2.0 * SPACING)
    grad_y = (y_next(rho, halo[3]) - y_prev(rho, halo[2])) / (2.0 * SPACING)
    grad_z = (z_next(rho) - z_prev(rho)) / (2.0 * SPACING)
    sigma = grad_x * grad_x + grad_y * grad_y + grad_z * grad_z
    n_sq = rho * rho + core[...] * core[...]
    third = jnp.exp(jnp.log(n_sq) * (1.0 / 6.0))
    smooth = jnp.sqrt(n_sq)
    four_thirds = smooth * third
    s2 = sigma / (4.0 * FERMI_SQ * four_thirds * four_thirds)
    denom = 1.0 + MU * s2 / KAPPA
    enhance = 1.0 + KAPPA - KAPPA / denom
    slope = MU / (denom * denom)
    de_dn = -AMPLITUDE * third * ((4.0 / 3.0) * enhance - (8.0 / 3.0) * s2 * slope)
    de_dsigma = -AMPLITUDE * slope / (4.0 * FERMI_SQ * four_thirds)
    flux_x = 2.0 * de_dsigma * grad_x
    flux_y = 2.0 * de_dsigma * grad_y
    flux_z = 2.0 * de_dsigma * grad_z
    flux[0] = flux_x
    flux[1] = flux_y
    for n in range(4):
        halo_copy(flux.at[n // 2], halo2, 4, n).start()
    partial = de_dn * rho / smooth + (z_prev(flux_z) - z_next(flux_z)) / (2.0 * SPACING)
    for n in range(4):
        halo_copy(flux.at[n // 2], halo2, 4, n).wait_recv()
    divergence = (
        x_prev(flux_x, halo2[0])
        - x_next(flux_x, halo2[1])
        + y_prev(flux_y, halo2[2])
        - y_next(flux_y, halo2[3])
    )
    pot[...] = partial + divergence / (2.0 * SPACING)

    def halo_sent():
        for n in range(4):
            halo_copy(charge, halo, 0, n).wait_send()
            halo_copy(flux.at[n // 2], halo2, 4, n).wait_send()

    parts[9 * tiles] = jnp.zeros((ob, ob), jnp.bfloat16)

    def part_step(t, carry):
        values = phi[t]
        weighted = (values.astype(jnp.float32) * pot[pl.ds(t, 1), :]).astype(jnp.bfloat16)
        block = lax.dot_general(
            weighted, values, (((1,), (1,)), ((), ())), preferred_element_type=jnp.float32
        ).astype(jnp.bfloat16)
        for a in range(3):
            for b in range(3):
                parts[9 * t + 3 * a + b] = block[ob * a : ob * a + ob, ob * b : ob * b + ob]
        return carry

    lax.fori_loop(0, tiles, part_step, 0, unroll=4)

    def rx_copy(j, way):
        return remote(rsend.at[way, j], (rleft, rright)[way].at[j], rx_sem, (way, j), (xr, xl)[way])

    def rf_copy(j, way):
        return remote(
            (rleft, rright)[way].at[j, 4], (rfleft, rfright)[way].at[j], rf_sem, (way, j), (xr, xl)[way]
        )

    def rz_copy(chain, k, way, lo=0, hi=4):
        rows = pl.ds(lo, hi - lo)
        return remote(
            zout.at[way, k, chain, rows], zin.at[way, k, chain, rows], rz_sem, (chain, way, k), (zup, zdn)[way]
        )

    def give(j):
        slots = (((1, 0), (1, 1), (2, 0)), ((3, 0), (3, 1), (2, 1)))
        for way in range(2):
            for n, (dx, seat) in enumerate(slots[way]):
                pair = pair_of(dx, j, seat)
                if n < 2:
                    rsend[way, j, 2 * n] = parts[pair, :hb, :]
                    rsend[way, j, 2 * n + 1] = parts[pair, hb:, :]
                else:
                    rsend[way, j, 4] = parts[pair, hb:, :]
            rx_copy(j, way).start()

    def pass_on(j):
        for way in range(2):
            rx_copy(j, way).wait_recv()
            rf_copy(j, way).start()

    def by_source(pieces, j):
        total = [jnp.zeros((ROWS, ob), jnp.float32)] * 4
        for ref, dx, seat, piece in pieces:
            src = ref[pl.ds(dx * span + 2 * j + seat, 1), :]
            piece = piece.astype(jnp.float32)
            total = [t + jnp.where(src == s, piece, 0.0) for s, t in enumerate(total)]
        return total

    def summed(j, chain, lo):
        rows = pl.ds(lo, ROWS)
        if chain == 2:
            return by_source(
                [(req, 2, s, parts[pair_of(2, j, s), rows, :]) for s in range(2)], j
            )
        pieces = [
            (req, 0, s, parts[pair_of(0, j, s), pl.ds(hb * chain + lo, ROWS), :]) for s in range(2)
        ]
        for s in range(2):
            pieces.append((want, 1, s, rleft[j, 2 * s + chain, rows, :]))
            pieces.append((want, 3, s, rright[j, 2 * s + chain, rows, :]))
        if chain == 1:
            pieces.append((want, 2, 0, rfleft[j, rows, :]))
            pieces.append((want, 2, 1, rfright[j, rows, :]))
        return by_source(pieces, j)

    def arrived(j):
        for way in range(2):
            rf_copy(j, way).wait_recv()

    def rz_first(chain):
        for lo in range(0, hb, ROWS):
            total = summed(half, chain, lo)
            for s in range(4):
                zout[s // 2, 0, chain, s, pl.ds(lo, ROWS), :] = total[s].astype(jnp.bfloat16)
        for way in range(2):
            rz_copy(chain, 0, way, 2 * way, 2 * way + 2).start()

    def rz_arrived(chain, k, way):
        @pl.when(k == 0)
        def _():
            rz_copy(chain, 0, way, 2 * way, 2 * way + 2).wait_recv()

        @pl.when(k > 0)
        def _():
            rz_copy(chain, k, way).wait_recv()

    def rz_step(chain, k, way):
        j = half - k if way == 0 else half + k
        rz_arrived(chain, k - 1, way)
        for lo in range(0, hb, ROWS):
            rows = pl.ds(lo, ROWS)
            total = summed(j, chain, lo)
            for s in range(4):
                value = total[s] + zin[way, k - 1, chain, s, rows, :].astype(jnp.float32)
                zout[way, k, chain, s, rows, :] = value.astype(jnp.bfloat16)
        rz_copy(chain, k, way).start()

    def rz_final(chain, lo):
        rows = pl.ds(lo, ROWS)
        return [
            t + zin[0, half - 1, chain, s, rows, :].astype(jnp.float32)
            + zin[1, half - 1, chain, s, rows, :].astype(jnp.float32)
            for s, t in enumerate(summed(0, chain, lo))
        ]

    for chain in range(3):
        for s in range(2):
            zin[0, 0, chain, 2 + s] = jnp.zeros((hb, ob), jnp.bfloat16)
            zin[1, 0, chain, s] = jnp.zeros((hb, ob), jnp.bfloat16)
    give(half)
    rz_first(2)
    give(half - 1)
    give(half + 1)
    pass_on(half)
    rz_first(0)
    give(half - 2)
    give(half + 2)
    for way in range(2):
        rz_step(2, 1, way)
    pass_on(half - 1)
    pass_on(half + 1)
    arrived(half)
    rz_first(1)
    far_sum_copy = remote(far_out, far_in, want_sem, (4,), x2)

    def reduce_step(k, carry):
        @pl.when(k < half - 2)
        def _():
            give(half - k - 2)
            give(half + k + 2)

        @pl.when(k == half - 2)
        def _():
            give(0)

        for way in range(2):
            rz_step(0, k, way)

        @pl.when(k < half - 1)
        def _():
            for way in range(2):
                rz_step(2, k + 1, way)
            pass_on(half - k - 1)
            pass_on(half + k + 1)

        @pl.when(k == half - 1)
        def _():
            for way in range(2):
                rz_arrived(2, half - 1, way)
            for lo in range(0, hb, ROWS):
                for s, value in enumerate(rz_final(2, lo)):
                    far_out[s, pl.ds(lo, ROWS), :] = value.astype(jnp.bfloat16)
            far_sum_copy.start()
            pass_on(0)

        for way in range(2):
            arrived(half - k if way == 0 else half + k)
            rz_step(1, k, way)
        return carry

    lax.fori_loop(1, half, reduce_step, 0)

    for way in range(2):
        lnv_copy(turn - 1, way).wait_recv()
    for n in range(4):
        slab = jnp.zeros((8, 128), jnp.float32)
        for t in range(tiles):
            points_t = jnp.broadcast_to(pot[pl.ds(t, 1), pl.ds(128 * n, 128)], (8, 128))
            slab = jnp.where(group[:8] == t, spread(jnp.where(own_group, points_t, 0.0)), slab)
        pot_out[pl.ds(8 * n, 8), :] = slab[:, : 16 * tiles]

    pot_save = pltpu.make_async_copy(pot_out, pot_hbm, out_sem.at[0])
    pot_save.start()

    def left_step(n, carry):
        for t in range(8):
            slot = term_left[lax.div(n, 2), lax.rem(n, 2), t]
            column = lax.rem(lax.shift_right_logical(slot, 1) + cols - c, cols)
            lnv_cat[n, :, pl.ds(ob * t, ob)] = lnv_all[column * 4 + lax.div(n, 2) * 2 + (slot & 1)]
        return carry

    lax.fori_loop(0, 4, left_step, 0)
    arrived(0)
    for way in range(2):
        rz_arrived(0, half - 1, way)
        rz_arrived(1, half - 1, way)
    far_sum_copy.wait_recv()
    for chain in range(2):
        for lo in range(0, hb, ROWS):
            rows = pl.ds(hb * chain + lo, ROWS)
            for s, value in enumerate(rz_final(chain, lo)):
                if chain == 0:
                    value = value + far_in[s, pl.ds(lo, ROWS), :].astype(jnp.float32)
                ham_out[s, rows, :] = value
                ham_half[s, rows, :] = value.astype(jnp.bfloat16)

    def reduce_sent():
        def sent_x(j, carry):
            for way in range(2):
                rx_copy(j, way).wait_send()
                rf_copy(j, way).wait_send()
            return carry

        def sent_z(k, carry):
            for chain in range(3):
                for way in range(2):
                    rz_copy(chain, k, way).wait_send()
            return carry

        for chain in range(3):
            for way in range(2):
                rz_copy(chain, 0, way, 2 * way, 2 * way + 2).wait_send()
        far_sum_copy.wait_send()
        lax.fori_loop(0, depth, sent_x, 0)
        lax.fori_loop(1, half, sent_z, 0)

    def win_copy(src, dst, first, n):
        return remote(src, dst.at[pl.ds(8 * n, 4)], win_sem, (first + n,), (wp, wm)[n])

    def win_block(s, n):
        return remote(first_half.at[s], window2.at[8 * n + s], win_sem, (2 + 2 * s + n,), (wp, wm)[n])

    def product(n, win):
        chosen = jnp.concatenate([win[term_right[n // 2, n % 2, t]] for t in range(8)], axis=0)
        return jnp.dot(lnv_cat[n], chosen, preferred_element_type=jnp.float32)

    for n in range(2):
        win_copy(ham_half, window, 0, n).start()
    ham_save = pltpu.make_async_copy(ham_out, ham_hbm, out_sem.at[1])
    ham_save.start()
    for s in range(4):
        window[4 + s] = ham_half[s]
    for n in range(2):
        win_copy(ham_half, window, 0, n).wait_recv()
    for s in range(4):
        first = product(s, window)
        grad_out[s] = first
        first_half[s] = first.astype(jnp.bfloat16)
        for n in range(2):
            win_block(s, n).start()
    for s in range(4):
        window2[4 + s] = first_half[s]
    for s in range(4):
        for n in range(2):
            win_block(s, n).wait_recv()
    saves = [pot_save, ham_save]
    for s in range(4):
        grad_out[s] = 3.0 * grad_out[s] - 2.0 * product(s, window2)
        saves.append(pltpu.make_async_copy(grad_out.at[s], grad_hbm.at[s], out_sem.at[2 + s]))
        saves[-1].start()

    gather_sent()
    halo_sent()
    reduce_sent()
    for save in saves:
        save.wait()
    for n in range(2):
        win_copy(ham_half, window, 0, n).wait_send()
        for s in range(4):
            win_block(s, n).wait_send()


def save_kernel(*refs):
    sources, results, held, sems = refs[:3], refs[3:6], refs[6:9], refs[9]
    loads = [pltpu.make_async_copy(sources[n], held[n], sems.at[0, n]) for n in range(3)]
    saves = [pltpu.make_async_copy(held[n], results[n], sems.at[1, n]) for n in range(3)]
    for load in loads:
        load.start()
    for load, save in zip(loads, saves):
        load.wait()
        save.start()
    for save in saves:
        save.wait()


def body(phi_values, density, lnv_matrix, core_density, pair_owner, pair_source, term_left, term_right):
    phi = phi_values[0, 0]
    tiles, _, points = phi.shape
    ob = density.shape[-1]
    depth = lax.axis_size("wide") // NX
    cols = lax.axis_size("col")
    half = depth // 2
    slabs, strips, deep = core_density.shape
    slots = 2 * NX * depth
    shapes = tuple(
        jax.ShapeDtypeStruct(shape, jnp.float32) for shape in ((slabs * strips, deep), (4, ob, ob), (4, ob, ob))
    )
    block = lambda *n: pltpu.VMEM((*n, ob, ob), jnp.bfloat16)
    halves = lambda *n: pltpu.VMEM((*n, ob // 2, ob), jnp.bfloat16)
    sems = lambda *n: pltpu.SemaphoreType.DMA((2, *n))
    smem = pl.BlockSpec(memory_space=pltpu.SMEM)
    hbm = pl.BlockSpec(memory_space=pltpu.HBM)
    outs = pl.pallas_call(
        functools.partial(step_kernel, depth),
        out_shape=shapes,
        in_specs=[smem] * 2 + [hbm] * 6,
        out_specs=(hbm, hbm, hbm),
        scratch_shapes=[
            *[pltpu.VMEM(shape.shape, jnp.float32) for shape in shapes],
            pltpu.VMEM((1, 9 * tiles), jnp.int32),
            pltpu.VMEM((1, 9 * tiles), jnp.int32),
            pltpu.VMEM((slabs * strips, deep), jnp.float32),
            pltpu.VMEM((tiles, points), jnp.float32),
            pltpu.VMEM(phi.shape, jnp.bfloat16),
            pltpu.VMEM((8, 128), jnp.int32),
            pltpu.SMEM((8, 128), jnp.int32),
            pltpu.VMEM((slots, ob), jnp.int32),
            pltpu.VMEM((slots, ob), jnp.int32),
            halves(24 * depth),
            halves(2, depth, 5),
            block(9 * tiles + 1),
            halves(2, depth, 5),
            halves(depth, 5),
            halves(depth, 5),
            halves(depth),
            halves(depth),
            halves(2, half, 3, 4),
            halves(2, half, 3, 4),
            halves(4),
            halves(4),
            block(4 * cols),
            pltpu.VMEM((4, ob, 8 * ob), jnp.bfloat16),
            pltpu.VMEM((3 * ob, 3 * ob), jnp.bfloat16),
            pltpu.VMEM((tiles, points), jnp.float32),
            pltpu.VMEM((4, tiles, points), jnp.float32),
            pltpu.VMEM((2, tiles, points), jnp.float32),
            pltpu.VMEM((4, tiles, points), jnp.float32),
            pltpu.VMEM((tiles, points), jnp.float32),
            block(12),
            block(12),
            block(4),
            block(4),
            pltpu.SemaphoreType.DMA((8,)),
            sems(5),
            sems(2, cols // 2),
            sems(3, 2, half),
            sems(2, depth),
            sems(2, depth),
            sems(2, depth),
            sems(2, depth),
            sems(3, 2, half),
            sems(8),
            sems(10),
            pltpu.SemaphoreType.DMA((6,)),
        ],
        compiler_params=pltpu.CompilerParams(
            collective_id=0, has_side_effects=True, vmem_limit_bytes=VMEM_BYTES
        ),
    )(
        term_left,
        term_right,
        pair_owner.reshape(1, 9 * tiles),
        pair_source.reshape(1, 9 * tiles),
        density.reshape(4, 2, ob // 2, ob),
        lnv_matrix.reshape(4, ob, ob),
        core_density.reshape(slabs * strips, deep),
        phi,
    )
    pot, ham, grad = pl.pallas_call(
        save_kernel,
        out_shape=shapes,
        in_specs=[hbm] * 3,
        out_specs=(hbm, hbm, hbm),
        scratch_shapes=[*[pltpu.VMEM(shape.shape, jnp.float32) for shape in shapes], sems(3)],
    )(*outs)
    return pot.reshape(core_density.shape), ham.reshape(density.shape), grad.reshape(density.shape)


def solution(mesh):
    grid = lambda n: P("wide", "col", *([None] * n))
    return jax.shard_map(
        body,
        mesh=mesh,
        in_specs=(grid(3), grid(2), grid(2), grid(1), grid(2), grid(1), grid(1), grid(1)),
        out_specs=(grid(1), grid(2), grid(2)),
        check_vma=False,
    )
```

```python
import functools
import math

import jax
import jax.numpy as jnp
from jax import lax
from jax.experimental import pallas as pl
from jax.experimental.pallas import tpu as pltpu
from jax.sharding import PartitionSpec as P

MESH = pl.DeviceIdType.MESH
NX = 4
SPACING = 0.1
KAPPA = 0.804
MU = 0.2195
FERMI_SQ = (3.0 * math.pi**2) ** (2.0 / 3.0)
AMPLITUDE = 0.75 * (3.0 / math.pi) ** (1.0 / 3.0)
VMEM_BYTES = 63 * 2**20
ROWS = 32


def pair_places(owner, source, z, x, depth):
    pairs = owner.shape[1]
    slots = 2 * NX * depth
    row = lax.broadcasted_iota(jnp.int32, (pairs, pairs), 0)
    lane = lax.broadcasted_iota(jnp.int32, (pairs, pairs), 1)
    along = owner
    down = jnp.sum(jnp.where(row == lane, along, 0), axis=1, keepdims=True)
    seat = jnp.sum(jnp.where((down == along) & (row < lane), 1, 0), axis=0, keepdims=True)
    seat = jnp.minimum(seat, 1)
    dz = lax.shift_right_logical(along, 2) - z
    dz = jnp.where(dz < 0, dz + depth, dz)
    dx = (along & 3) - x
    dx = jnp.where(dx < 0, dx + NX, dx)
    slot = dx * (2 * depth) + dz * 2 + seat
    hit = slot == lax.broadcasted_iota(jnp.int32, (slots, pairs), 0)
    slot_source = jnp.sum(jnp.where(hit, source + 1, 0), axis=1, keepdims=True) - 1
    slot_down = jnp.sum(jnp.where(row == lane, slot, 0), axis=1, keepdims=True)
    place = lax.broadcasted_iota(jnp.int32, (pairs, 128), 0)
    hit = slot_down == lax.broadcasted_iota(jnp.int32, (pairs, 128), 1)
    slot_pair = jnp.min(jnp.where(hit, place, pairs), axis=0, keepdims=True)
    halves = []
    for part in range(2):
        near = dz * 5 + seat * 2 + part
        far = 18 * depth + seat * depth + dz if part else 20 * depth + dz * 4 + source
        halves.append(
            jnp.where(
                dx == 0,
                dz * 8 + part * 4 + source,
                jnp.where(dx == 3, 8 * depth + near, jnp.where(dx == 1, 13 * depth + near, far)),
            )
        )
    return slot_source, slot_pair, halves


def step_kernel(
    depth,
    term_left,
    term_right,
    owner_hbm,
    source_hbm,
    dens_hbm,
    lnv_hbm,
    core_hbm,
    phi_hbm,
    pot_hbm,
    ham_hbm,
    grad_hbm,
    pot_out,
    ham_out,
    grad_out,
    owner,
    source,
    core_field,
    core,
    phi,
    places,
    index,
    req,
    want,
    buf,
    xsend,
    parts,
    rsend,
    rleft,
    rright,
    rfleft,
    rfright,
    zin,
    zout,
    far_in,
    far_out,
    lnv_all,
    lnv_cat,
    tile_matrix,
    charge,
    halo,
    flux,
    halo2,
    pot,
    window,
    window2,
    ham_half,
    first_half,
    load_sem,
    want_sem,
    lnv_sem,
    z_sem,
    x_sem,
    f_sem,
    rx_sem,
    rf_sem,
    rz_sem,
    halo_sem,
    win_sem,
    out_sem,
):
    w = lax.axis_index("wide")
    c = lax.axis_index("col")
    wides = depth * NX
    cols = lax.axis_size("col")
    tiles = charge.shape[0]
    half = depth // 2
    ob = phi.shape[1] // 3
    hb = ob // 2
    z, x = lax.div(w, NX), lax.rem(w, NX)

    def chip(dz, dx):
        return (lax.rem(z + depth + dz, depth) * NX + lax.rem(x + NX + dx, NX), c)

    slots = 2 * NX * depth
    zup, zdn, xr, xl, x2 = chip(1, 0), chip(-1, 0), chip(0, 1), chip(0, -1), chip(0, 2)
    wp = (lax.rem(w + 1, wides), c)
    wm = (lax.rem(w + wides - 1, wides), c)
    cp, cm = (w, lax.rem(c + 1, cols)), (w, lax.rem(c + cols - 1, cols))

    def remote(src, dst, sems, index, device):
        return pltpu.make_async_remote_copy(
            src_ref=src,
            dst_ref=dst,
            send_sem=sems.at[(0, *index)],
            recv_sem=sems.at[(1, *index)],
            device_id=device,
            device_id_type=MESH,
        )

    barrier = pltpu.get_barrier_semaphore()
    greeted = [zup, zdn, xr, xl, x2, wp, wm, cp, cm]
    for device in greeted:
        pl.semaphore_signal(barrier, inc=1, device_id=device, device_id_type=MESH)

    loads = [
        pltpu.make_async_copy(src, dst, load_sem.at[n])
        for n, (src, dst) in enumerate(
            (
                (owner_hbm, owner),
                (source_hbm, source),
                (dens_hbm.at[:, 0], buf.at[pl.ds(0, 4)]),
                (dens_hbm.at[:, 1], buf.at[pl.ds(4, 4)]),
                (lnv_hbm, lnv_all.at[pl.ds(0, 4)]),
                (core_hbm, core_field),
                (phi_hbm, phi),
            )
        )
    ]
    for load in loads:
        load.start()
    loads[0].wait()
    loads[1].wait()
    slot_source, slot_pair_row, halves = pair_places(owner[...], source[...], z, x, depth)
    req[...] = jnp.broadcast_to(slot_source, req.shape)
    want[pl.ds(0, 2 * depth), :] = req[pl.ds(0, 2 * depth), :]
    places[...] = jnp.zeros_like(places)
    places[pl.ds(0, 1), :] = slot_pair_row
    for part in range(2):
        places[pl.ds(1 + part, 1), pl.ds(0, 9 * tiles)] = halves[part]
    index_copy = pltpu.make_async_copy(places, index, load_sem.at[7])
    index_copy.start()

    def pair_of(dx, j, seat):
        return index[0, dx * span + 2 * j + seat]

    loads[2].wait()
    loads[3].wait()
    pl.semaphore_wait(barrier, len(greeted))

    left0, right0, fleft0, fright0, far0 = 8 * depth, 13 * depth, 18 * depth, 19 * depth, 20 * depth
    span = 2 * depth

    def z_copy(chain, k, way, lo=0, hi=4):
        stride, base = (8, 0) if chain == 0 else (8, 4) if chain == 1 else (4, far0)
        if way == 0:
            src, dst = lax.rem(depth - k, depth), depth - k - 1
        else:
            src, dst = k, k + 1
        return remote(
            buf.at[pl.ds(stride * src + base + lo, hi - lo)],
            buf.at[pl.ds(stride * dst + base + lo, hi - lo)],
            z_sem, (chain, way, k), (zup, zdn)[way],
        )

    def z_first(chain):
        for way in range(2):
            z_copy(chain, 0, way).start()

    def z_step(chain, k):
        for way in range(2):
            z_copy(chain, k - 1, way).wait_recv()
            z_copy(chain, k, way).start()

    def z_half(chain):
        for way in range(2):
            z_copy(chain, half - 2, way).wait_recv()
            z_copy(chain, half - 1, way, 2 * way, 2 * way + 2).start()

    def z_last(chain):
        for way in range(2):
            z_copy(chain, half - 1, way, 2 * way, 2 * way + 2).wait_recv()

    def x_copy(j, way):
        if way == 0:
            return remote(xsend.at[0, j], buf.at[pl.ds(left0 + 5 * j, 5)], x_sem, (0, j), xr)
        return remote(xsend.at[1, j], buf.at[pl.ds(right0 + 5 * j, 5)], x_sem, (1, j), xl)

    def f_copy(j, way):
        if way == 0:
            return remote(buf.at[left0 + 5 * j + 4], buf.at[fleft0 + j], f_sem, (0, j), xr)
        return remote(buf.at[right0 + 5 * j + 4], buf.at[fright0 + j], f_sem, (1, j), xl)

    def pack(j):
        wanted = (((3, 0), (3, 1), (2, 0)), ((1, 0), (1, 1), (2, 1)))
        for h in range(2):
            for lo in range(0, hb, ROWS):
                rows = pl.ds(lo, ROWS)
                b = [buf[8 * j + 4 * h + s, rows, :].astype(jnp.float32) for s in range(4)]
                for way in range(2):
                    for n, (dx, seat) in enumerate(wanted[way]):
                        if n == 2 and h == 0:
                            continue
                        src = want[pl.ds(dx * span + 2 * j + seat, 1), :]
                        got = jnp.where(
                            src == 0, b[0], jnp.where(src == 1, b[1], jnp.where(src == 2, b[2], b[3]))
                        )
                        xsend[way, j, 4 if n == 2 else 2 * n + h, rows, :] = got.astype(jnp.bfloat16)
        for way in range(2):
            x_copy(j, way).start()

    def forward(j):
        for way in range(2):
            x_copy(j, way).wait_recv()
            f_copy(j, way).start()

    def want_copy(dx, device):
        rows = pl.ds(dx * span, span)
        return remote(req.at[rows], want.at[rows], want_sem, (dx,), device)

    want_copies = [want_copy(1, xr), want_copy(3, xl), want_copy(2, x2)]
    for copy in want_copies:
        copy.start()
    far_copy = remote(buf.at[pl.ds(0, 4)], buf.at[pl.ds(far0, 4)], want_sem, (0,), x2)
    far_copy.start()
    z_first(0)
    z_first(1)

    turn = cols // 2

    def lnv_copy(k, way):
        lo, n = (2 * way, 2) if k == turn - 1 else (0, 4)
        src, dst = ((cols - k) % cols, cols - k - 1) if way == 0 else (k, k + 1)
        return remote(
            lnv_all.at[pl.ds(4 * src + lo, n)], lnv_all.at[pl.ds(4 * dst + lo, n)], lnv_sem, (way, k), (cp, cm)[way]
        )

    loads[4].wait()
    for way in range(2):
        lnv_copy(0, way).start()
    for copy in want_copies:
        copy.wait_recv()
    pack(0)
    far_copy.wait_recv()
    z_first(2)

    def gather_step(k, carry):
        z_step(0, k)
        z_step(1, k)
        pack(depth - k)
        pack(k)
        z_step(2, k)
        for n in range(1, turn):

            @pl.when(k == n + 1)
            def _():
                for way in range(2):
                    lnv_copy(n - 1, way).wait_recv()
                    lnv_copy(n, way).start()

        @pl.when(k == 1)
        def _():
            forward(0)

        @pl.when(k > 1)
        def _():
            forward(depth - k + 1)
            forward(k - 1)

        return carry

    lax.fori_loop(1, half - 1, gather_step, 0)
    z_half(0)
    z_half(1)
    pack(half + 1)
    pack(half - 1)
    z_half(2)
    for k in range(half - 2, half - 1):
        if k == 0:
            forward(0)
        elif k > 0:
            forward(depth - k)
            forward(k)
    z_last(0)
    z_last(1)
    pack(half)
    forward(half + 1)
    forward(half - 1)
    forward(half)
    z_last(2)

    def gather_end(j, carry):
        for way in range(2):
            f_copy(j, way).wait_recv()
        return carry

    loads[5].wait()
    field = core_field[...]
    if field.shape[1] < 128:
        field = jnp.pad(field, ((0, 0), (0, 128 - field.shape[1])))
    group = lax.div(lax.broadcasted_iota(jnp.int32, (32, 128), 1), 16)
    own_group = group[:8] == lax.broadcasted_iota(jnp.int32, (8, 128), 0)

    def spread(a):
        for shift in (64, 32, 16):
            a = a + pltpu.roll(a, shift, 1)
        return a

    for t in range(tiles):
        every = spread(jnp.where(group == t, field, 0.0))
        for n in range(4):
            chosen = jnp.where(own_group, every[8 * n : 8 * n + 8], 0.0)
            core[pl.ds(t, 1), pl.ds(128 * n, 128)] = jnp.sum(chosen, axis=0, keepdims=True)
    lax.fori_loop(0, depth, gather_end, 0)
    loads[6].wait()
    index_copy.wait()

    def gather_sent():
        def sent_x(j, carry):
            for way in range(2):
                x_copy(j, way).wait_send()
                f_copy(j, way).wait_send()
            return carry

        def sent_z(k, carry):
            for chain in range(3):
                for way in range(2):
                    z_copy(chain, k, way).wait_send()
            return carry

        for copy in want_copies:
            copy.wait_send()
        far_copy.wait_send()
        for k in range(turn):
            for way in range(2):
                lnv_copy(k, way).wait_send()
        for chain in range(3):
            for way in range(2):
                z_copy(chain, half - 1, way, 2 * way, 2 * way + 2).wait_send()
        lax.fori_loop(0, depth, sent_x, 0)
        lax.fori_loop(0, half - 1, sent_z, 0)


    def charge_step(t, carry):
        for a in range(3):
            for b in range(3):
                for h in range(2):
                    tile_matrix[pl.ds(ob * a + hb * h, hb), pl.ds(ob * b, ob)] = buf[
                        index[1 + h, 9 * t + 3 * a + b]
                    ]
        values = phi[t]
        applied = jnp.dot(tile_matrix[...], values, preferred_element_type=jnp.float32)
        charge[pl.ds(t, 1), :] = jnp.sum(values.astype(jnp.float32) * applied, axis=0, keepdims=True)
        return carry

    lax.fori_loop(0, tiles, charge_step, 0, unroll=4)

    sides = (wp, wm, cp, cm)

    def halo_copy(src, dst, first, n):
        return remote(src, dst.at[n], halo_sem, (first + n,), sides[n])

    for n in range(4):
        halo_copy(charge, halo, 0, n).start()

    points = charge.shape[1]
    xcell, ycell, zcell = points // 2, points // 32, 1
    lane = lax.broadcasted_iota(jnp.int32, (tiles, points), 1)
    at_x = lax.div(lane, xcell)
    at_y = lax.rem(lax.div(lane, ycell), 16)
    at_z = lax.rem(lane, 16)

    def turned(a, shift):
        return pltpu.roll(a, shift % points, 1)

    def x_next(a, beyond):
        return turned(jnp.where(at_x == 1, a, beyond), xcell)

    def x_prev(a, beyond):
        return turned(jnp.where(at_x == 0, a, beyond), xcell)

    def y_next(a, beyond):
        return jnp.where(at_y < 15, turned(a, -ycell), turned(beyond, 15 * ycell))

    def y_prev(a, beyond):
        return jnp.where(at_y > 0, turned(a, ycell), turned(beyond, -15 * ycell))

    def z_next(a):
        return jnp.where(at_z < 15, turned(a, -1), turned(pltpu.roll(a, tiles - 1, 0), 15))

    def z_prev(a):
        return jnp.where(at_z > 0, turned(a, 1), turned(pltpu.roll(a, 1, 0), -15))

    rho = charge[...]
    for n in range(4):
        halo_copy(charge, halo, 0, n).wait_recv()
    grad_x = (x_next(rho, halo[1]) - x_prev(rho, halo[0])) / (2.0 * SPACING)
    grad_y = (y_next(rho, halo[3]) - y_prev(rho, halo[2])) / (2.0 * SPACING)
    grad_z = (z_next(rho) - z_prev(rho)) / (2.0 * SPACING)
    sigma = grad_x * grad_x + grad_y * grad_y + grad_z * grad_z
    n_sq = rho * rho + core[...] * core[...]
    third = jnp.exp(jnp.log(n_sq) * (1.0 / 6.0))
    smooth = jnp.sqrt(n_sq)
    four_thirds = smooth * third
    s2 = sigma / (4.0 * FERMI_SQ * four_thirds * four_thirds)
    denom = 1.0 + MU * s2 / KAPPA
    enhance = 1.0 + KAPPA - KAPPA / denom
    slope = MU / (denom * denom)
    de_dn = -AMPLITUDE * third * ((4.0 / 3.0) * enhance - (8.0 / 3.0) * s2 * slope)
    de_dsigma = -AMPLITUDE * slope / (4.0 * FERMI_SQ * four_thirds)
    flux_x = 2.0 * de_dsigma * grad_x
    flux_y = 2.0 * de_dsigma * grad_y
    flux_z = 2.0 * de_dsigma * grad_z
    flux[0] = flux_x
    flux[1] = flux_y
    for n in range(4):
        halo_copy(flux.at[n // 2], halo2, 4, n).start()
    partial = de_dn * rho / smooth + (z_prev(flux_z) - z_next(flux_z)) / (2.0 * SPACING)
    for n in range(4):
        halo_copy(flux.at[n // 2], halo2, 4, n).wait_recv()
    divergence = (
        x_prev(flux_x, halo2[0])
        - x_next(flux_x, halo2[1])
        + y_prev(flux_y, halo2[2])
        - y_next(flux_y, halo2[3])
    )
    pot[...] = partial + divergence / (2.0 * SPACING)

    def halo_sent():
        for n in range(4):
            halo_copy(charge, halo, 0, n).wait_send()
            halo_copy(flux.at[n // 2], halo2, 4, n).wait_send()

    parts[9 * tiles] = jnp.zeros((ob, ob), jnp.bfloat16)

    def part_step(t, carry):
        values = phi[t]
        weighted = (values.astype(jnp.float32) * pot[pl.ds(t, 1), :]).astype(jnp.bfloat16)
        block = lax.dot_general(
            weighted, values, (((1,), (1,)), ((), ())), preferred_element_type=jnp.float32
        ).astype(jnp.bfloat16)
        for a in range(3):
            for b in range(3):
                parts[9 * t + 3 * a + b] = block[ob * a : ob * a + ob, ob * b : ob * b + ob]
        return carry

    lax.fori_loop(0, tiles, part_step, 0, unroll=4)

    def rx_copy(j, way):
        return remote(rsend.at[way, j], (rleft, rright)[way].at[j], rx_sem, (way, j), (xr, xl)[way])

    def rf_copy(j, way):
        return remote(
            (rleft, rright)[way].at[j, 4], (rfleft, rfright)[way].at[j], rf_sem, (way, j), (xr, xl)[way]
        )

    def rz_copy(chain, k, way, lo=0, hi=4):
        rows = pl.ds(lo, hi - lo)
        return remote(
            zout.at[way, k, chain, rows], zin.at[way, k, chain, rows], rz_sem, (chain, way, k), (zup, zdn)[way]
        )

    def give(j):
        slots = (((1, 0), (1, 1), (2, 0)), ((3, 0), (3, 1), (2, 1)))
        for way in range(2):
            for n, (dx, seat) in enumerate(slots[way]):
                pair = pair_of(dx, j, seat)
                if n < 2:
                    rsend[way, j, 2 * n] = parts[pair, :hb, :]
                    rsend[way, j, 2 * n + 1] = parts[pair, hb:, :]
                else:
                    rsend[way, j, 4] = parts[pair, hb:, :]
            rx_copy(j, way).start()

    def pass_on(j):
        for way in range(2):
            rx_copy(j, way).wait_recv()
            rf_copy(j, way).start()

    def by_source(pieces, j):
        total = [jnp.zeros((ROWS, ob), jnp.float32)] * 4
        for ref, dx, seat, piece in pieces:
            src = ref[pl.ds(dx * span + 2 * j + seat, 1), :]
            piece = piece.astype(jnp.float32)
            total = [t + jnp.where(src == s, piece, 0.0) for s, t in enumerate(total)]
        return total

    def summed(j, chain, lo):
        rows = pl.ds(lo, ROWS)
        if chain == 2:
            return by_source(
                [(req, 2, s, parts[pair_of(2, j, s), rows, :]) for s in range(2)], j
            )
        pieces = [
            (req, 0, s, parts[pair_of(0, j, s), pl.ds(hb * chain + lo, ROWS), :]) for s in range(2)
        ]
        for s in range(2):
            pieces.append((want, 1, s, rleft[j, 2 * s + chain, rows, :]))
            pieces.append((want, 3, s, rright[j, 2 * s + chain, rows, :]))
        if chain == 1:
            pieces.append((want, 2, 0, rfleft[j, rows, :]))
            pieces.append((want, 2, 1, rfright[j, rows, :]))
        return by_source(pieces, j)

    def arrived(j):
        for way in range(2):
            rf_copy(j, way).wait_recv()

    def rz_first(chain):
        for lo in range(0, hb, ROWS):
            total = summed(half, chain, lo)
            for s in range(4):
                zout[s // 2, 0, chain, s, pl.ds(lo, ROWS), :] = total[s].astype(jnp.bfloat16)
        for way in range(2):
            rz_copy(chain, 0, way, 2 * way, 2 * way + 2).start()

    def rz_arrived(chain, k, way):
        @pl.when(k == 0)
        def _():
            rz_copy(chain, 0, way, 2 * way, 2 * way + 2).wait_recv()

        @pl.when(k > 0)
        def _():
            rz_copy(chain, k, way).wait_recv()

    def rz_step(chain, k, way):
        j = half - k if way == 0 else half + k
        rz_arrived(chain, k - 1, way)
        for lo in range(0, hb, ROWS):
            rows = pl.ds(lo, ROWS)
            total = summed(j, chain, lo)
            for s in range(4):
                value = total[s] + zin[way, k - 1, chain, s, rows, :].astype(jnp.float32)
                zout[way, k, chain, s, rows, :] = value.astype(jnp.bfloat16)
        rz_copy(chain, k, way).start()

    def rz_final(chain, lo):
        rows = pl.ds(lo, ROWS)
        return [
            t + zin[0, half - 1, chain, s, rows, :].astype(jnp.float32)
            + zin[1, half - 1, chain, s, rows, :].astype(jnp.float32)
            for s, t in enumerate(summed(0, chain, lo))
        ]

    for chain in range(3):
        for s in range(2):
            zin[0, 0, chain, 2 + s] = jnp.zeros((hb, ob), jnp.bfloat16)
            zin[1, 0, chain, s] = jnp.zeros((hb, ob), jnp.bfloat16)
    give(half)
    rz_first(2)
    give(half - 1)
    give(half + 1)
    pass_on(half)
    rz_first(0)
    give(half - 2)
    give(half + 2)
    for way in range(2):
        rz_step(2, 1, way)
    pass_on(half - 1)
    pass_on(half + 1)
    arrived(half)
    rz_first(1)
    far_sum_copy = remote(far_out, far_in, want_sem, (4,), x2)

    def reduce_step(k, carry):
        @pl.when(k < half - 2)
        def _():
            give(half - k - 2)
            give(half + k + 2)

        @pl.when(k == half - 2)
        def _():
            give(0)

        for way in range(2):
            rz_step(0, k, way)

        @pl.when(k < half - 1)
        def _():
            for way in range(2):
                rz_step(2, k + 1, way)
            pass_on(half - k - 1)
            pass_on(half + k + 1)

        @pl.when(k == half - 1)
        def _():
            for way in range(2):
                rz_arrived(2, half - 1, way)
            for lo in range(0, hb, ROWS):
                for s, value in enumerate(rz_final(2, lo)):
                    far_out[s, pl.ds(lo, ROWS), :] = value.astype(jnp.bfloat16)
            far_sum_copy.start()
            pass_on(0)

        for way in range(2):
            arrived(half - k if way == 0 else half + k)
            rz_step(1, k, way)
        return carry

    lax.fori_loop(1, half, reduce_step, 0)

    for way in range(2):
        lnv_copy(turn - 1, way).wait_recv()
    for n in range(4):
        slab = jnp.zeros((8, 128), jnp.float32)
        for t in range(tiles):
            points_t = jnp.broadcast_to(pot[pl.ds(t, 1), pl.ds(128 * n, 128)], (8, 128))
            slab = jnp.where(group[:8] == t, spread(jnp.where(own_group, points_t, 0.0)), slab)
        pot_out[pl.ds(8 * n, 8), :] = slab[:, : 16 * tiles]

    pot_save = pltpu.make_async_copy(pot_out, pot_hbm, out_sem.at[0])
    pot_save.start()

    def left_step(n, carry):
        for t in range(8):
            slot = term_left[lax.div(n, 2), lax.rem(n, 2), t]
            column = lax.rem(lax.shift_right_logical(slot, 1) + cols - c, cols)
            lnv_cat[n, :, pl.ds(ob * t, ob)] = lnv_all[column * 4 + lax.div(n, 2) * 2 + (slot & 1)]
        return carry

    lax.fori_loop(0, 4, left_step, 0)
    def win_copy(chain, n):
        rows = pl.ds(hb * chain, hb)
        return remote(
            ham_half.at[:, rows], window.at[pl.ds(8 * n, 4), rows], win_sem, (2 * chain + n,), (wp, wm)[n]
        )

    for chain in range(2):
        for way in range(2):
            rz_arrived(chain, half - 1, way)
        if chain == 0:
            far_sum_copy.wait_recv()
        else:
            arrived(0)
        for lo in range(0, hb, ROWS):
            rows = pl.ds(hb * chain + lo, ROWS)
            for s, value in enumerate(rz_final(chain, lo)):
                if chain == 0:
                    value = value + far_in[s, pl.ds(lo, ROWS), :].astype(jnp.float32)
                ham_out[s, rows, :] = value
                ham_half[s, rows, :] = value.astype(jnp.bfloat16)
        for n in range(2):
            win_copy(chain, n).start()

    def reduce_sent():
        def sent_x(j, carry):
            for way in range(2):
                rx_copy(j, way).wait_send()
                rf_copy(j, way).wait_send()
            return carry

        def sent_z(k, carry):
            for chain in range(3):
                for way in range(2):
                    rz_copy(chain, k, way).wait_send()
            return carry

        for chain in range(3):
            for way in range(2):
                rz_copy(chain, 0, way, 2 * way, 2 * way + 2).wait_send()
        far_sum_copy.wait_send()
        lax.fori_loop(0, depth, sent_x, 0)
        lax.fori_loop(1, half, sent_z, 0)

    def win_block(s, n):
        return remote(first_half.at[s], window2.at[8 * n + s], win_sem, (4 + 2 * s + n,), (wp, wm)[n])

    def product(n, win):
        chosen = jnp.concatenate([win[term_right[n // 2, n % 2, t]] for t in range(8)], axis=0)
        return jnp.dot(lnv_cat[n], chosen, preferred_element_type=jnp.float32)

    ham_save = pltpu.make_async_copy(ham_out, ham_hbm, out_sem.at[1])
    ham_save.start()
    for s in range(4):
        window[4 + s] = ham_half[s]
    for n in range(4):
        win_copy(n // 2, n % 2).wait_recv()
    for s in range(4):
        first = product(s, window)
        grad_out[s] = first
        first_half[s] = first.astype(jnp.bfloat16)
        for n in range(2):
            win_block(s, n).start()
    for s in range(4):
        window2[4 + s] = first_half[s]
    for s in range(4):
        for n in range(2):
            win_block(s, n).wait_recv()
    saves = [pot_save, ham_save]
    for s in range(4):
        grad_out[s] = 3.0 * grad_out[s] - 2.0 * product(s, window2)
        saves.append(pltpu.make_async_copy(grad_out.at[s], grad_hbm.at[s], out_sem.at[2 + s]))
        saves[-1].start()

    gather_sent()
    halo_sent()
    reduce_sent()
    for save in saves:
        save.wait()
    for n in range(2):
        for chain in range(2):
            win_copy(chain, n).wait_send()
        for s in range(4):
            win_block(s, n).wait_send()


def save_kernel(*refs):
    sources, results, held, sems = refs[:3], refs[3:6], refs[6:9], refs[9]
    loads = [pltpu.make_async_copy(sources[n], held[n], sems.at[0, n]) for n in range(3)]
    saves = [pltpu.make_async_copy(held[n], results[n], sems.at[1, n]) for n in range(3)]
    for load in loads:
        load.start()
    for load, save in zip(loads, saves):
        load.wait()
        save.start()
    for save in saves:
        save.wait()


def body(phi_values, density, lnv_matrix, core_density, pair_owner, pair_source, term_left, term_right):
    phi = phi_values[0, 0]
    tiles, _, points = phi.shape
    ob = density.shape[-1]
    depth = lax.axis_size("wide") // NX
    cols = lax.axis_size("col")
    half = depth // 2
    slabs, strips, deep = core_density.shape
    slots = 2 * NX * depth
    shapes = tuple(
        jax.ShapeDtypeStruct(shape, jnp.float32) for shape in ((slabs * strips, deep), (4, ob, ob), (4, ob, ob))
    )
    block = lambda *n: pltpu.VMEM((*n, ob, ob), jnp.bfloat16)
    halves = lambda *n: pltpu.VMEM((*n, ob // 2, ob), jnp.bfloat16)
    sems = lambda *n: pltpu.SemaphoreType.DMA((2, *n))
    smem = pl.BlockSpec(memory_space=pltpu.SMEM)
    hbm = pl.BlockSpec(memory_space=pltpu.HBM)
    outs = pl.pallas_call(
        functools.partial(step_kernel, depth),
        out_shape=shapes,
        in_specs=[smem] * 2 + [hbm] * 6,
        out_specs=(hbm, hbm, hbm),
        scratch_shapes=[
            *[pltpu.VMEM(shape.shape, jnp.float32) for shape in shapes],
            pltpu.VMEM((1, 9 * tiles), jnp.int32),
            pltpu.VMEM((1, 9 * tiles), jnp.int32),
            pltpu.VMEM((slabs * strips, deep), jnp.float32),
            pltpu.VMEM((tiles, points), jnp.float32),
            pltpu.VMEM(phi.shape, jnp.bfloat16),
            pltpu.VMEM((8, 128), jnp.int32),
            pltpu.SMEM((8, 128), jnp.int32),
            pltpu.VMEM((slots, ob), jnp.int32),
            pltpu.VMEM((slots, ob), jnp.int32),
            halves(24 * depth),
            halves(2, depth, 5),
            block(9 * tiles + 1),
            halves(2, depth, 5),
            halves(depth, 5),
            halves(depth, 5),
            halves(depth),
            halves(depth),
            halves(2, half, 3, 4),
            halves(2, half, 3, 4),
            halves(4),
            halves(4),
            block(4 * cols),
            pltpu.VMEM((4, ob, 8 * ob), jnp.bfloat16),
            pltpu.VMEM((3 * ob, 3 * ob), jnp.bfloat16),
            pltpu.VMEM((tiles, points), jnp.float32),
            pltpu.VMEM((4, tiles, points), jnp.float32),
            pltpu.VMEM((2, tiles, points), jnp.float32),
            pltpu.VMEM((4, tiles, points), jnp.float32),
            pltpu.VMEM((tiles, points), jnp.float32),
            block(12),
            block(12),
            block(4),
            block(4),
            pltpu.SemaphoreType.DMA((8,)),
            sems(5),
            sems(2, cols // 2),
            sems(3, 2, half),
            sems(2, depth),
            sems(2, depth),
            sems(2, depth),
            sems(2, depth),
            sems(3, 2, half),
            sems(8),
            sems(12),
            pltpu.SemaphoreType.DMA((6,)),
        ],
        compiler_params=pltpu.CompilerParams(
            collective_id=0, has_side_effects=True, vmem_limit_bytes=VMEM_BYTES
        ),
    )(
        term_left,
        term_right,
        pair_owner.reshape(1, 9 * tiles),
        pair_source.reshape(1, 9 * tiles),
        density.reshape(4, 2, ob // 2, ob),
        lnv_matrix.reshape(4, ob, ob),
        core_density.reshape(slabs * strips, deep),
        phi,
    )
    pot, ham, grad = pl.pallas_call(
        save_kernel,
        out_shape=shapes,
        in_specs=[hbm] * 3,
        out_specs=(hbm, hbm, hbm),
        scratch_shapes=[*[pltpu.VMEM(shape.shape, jnp.float32) for shape in shapes], sems(3)],
    )(*outs)
    return pot.reshape(core_density.shape), ham.reshape(density.shape), grad.reshape(density.shape)


def solution(mesh):
    grid = lambda n: P("wide", "col", *([None] * n))
    return jax.shard_map(
        body,
        mesh=mesh,
        in_specs=(grid(3), grid(2), grid(2), grid(1), grid(2), grid(1), grid(1), grid(1)),
        out_specs=(grid(1), grid(2), grid(2)),
        check_vma=False,
    )
```
